256 devices in a mesh: dp: 4 (over y_hi, core), ctx: 64 (over x, z, y_lo).
Axes of the slice: x: 4, y: 4 (y_hi: 2, y_lo: 2; y = y_hi * 2 + y_lo), z: 8, core: 2. Of those that a mesh axis runs over, the one named last changes fastest.
Arguments:
- queries: bfloat16 [32768, 1536], P(('dp', 'ctx')), parts along dimension 0, may hold values from -23 to 23
- keys: bfloat16 [32768, 128], P(('dp', 'ctx')), parts along dimension 0, may hold values from -6 to 6
- values: bfloat16 [32768, 128], P(('dp', 'ctx')), parts along dimension 0, may hold values from -6 to 6
- forward_out: bfloat16 [32768, 1536], P(('dp', 'ctx')), parts along dimension 0, may hold values from -6 to 6
- out_grad: bfloat16 [32768, 1536], P(('dp', 'ctx')), parts along dimension 0, may hold values from -24 to 24
- span_ids: int32 [512], P(('dp', 'ctx')), parts along dimension 0, may hold values from 0 to 127, as said below
Outputs:
- d_queries: bfloat16 [32768, 1536], P(('dp', 'ctx')), parts along dimension 0
- d_keys: float32 [32768, 128], P(('dp', 'ctx')), parts along dimension 0
- d_values: float32 [32768, 128], P(('dp', 'ctx')), parts along dimension 0
The draws below stay inside these ranges and needn't reach their ends.
There are 4 independent parts, one for each index of `dp`. The reference program is written for one: setup_inputs(seed, part) draws one part's arguments, and reference() takes and returns one part's arrays. A program takes and returns all parts, laid end to end along the dimension named above; each array names one. Nothing has to cross between parts.
Inputs may be any that keep to these rules, and one draw needn't show every extreme that they name: `span_ids`: each span number appears once, and the two entries of one device sum to 127.
All inputs are finite; a program needn't handle non-finite values.
Results may differ from the reference program's by a relative error of at most 0.0047.
Values may be sent and summed in bfloat16 or wider, within the bound.
No kernel may reach another device: no remote copies, remote signals or barrier semaphores. Data moves between devices by JAX's collectives and lax.ppermute only.
A program may use at most 64 MiB of HBM per device.

```python
import jax
import jax.numpy as jnp
from jax import lax

HEADS = 12
HEAD_DIM = 128
SPAN = 64
SPANS = 128
TOKENS = 8192


def draw_keys(key, part):
    key = jax.random.fold_in(key, 1)
    result = jnp.clip(jax.random.normal(jax.random.fold_in(key, 2), (TOKENS, HEAD_DIM), jnp.float32), -6.0, 6.0)
    return result.astype(jnp.bfloat16)


def draw_queries(key, part):
    key = jax.random.fold_in(key, 2)
    columns = HEADS * HEAD_DIM
    result = jnp.clip(2.0 * jax.random.normal(jax.random.fold_in(key, 2), (TOKENS, columns), jnp.float32), -12.0, 12.0)
    return result.astype(jnp.bfloat16)


def draw_span_ids(key, part):
    key = jax.random.fold_in(key, 3)
    pairs = SPANS // 2
    order = jax.random.permutation(jax.random.fold_in(key, 1), pairs)
    flips = jax.random.randint(jax.random.fold_in(key, 2), (pairs,), 0, 2)
    first = jnp.where(flips == 1, SPANS - 1 - order, order)
    return jnp.stack([first, SPANS - 1 - first], axis=1).reshape(-1).astype(jnp.int32)


def block_levels(rng, shape, cuts, smallest, top_value):
    gain = 1.0
    for position, shards_of in cuts:
        steps = jax.random.uniform(jax.random.fold_in(jax.random.fold_in(rng, 6), position), (shards_of,), jnp.float32, smallest / len(cuts), top_value / len(cuts))
        gain = gain * jnp.repeat(jnp.exp(steps), shape[position] // shards_of).reshape((-1,) + (1,) * (len(shape) - 1 - position))
    return gain


def gaussian(rng, shape, deviation, most, pieces=(), held_as=jnp.bfloat16):
    entries = jax.random.normal(rng, shape, jnp.float32) * deviation
    if len(pieces) > 0:
        entries = block_levels(rng, shape, pieces, -0.22, 0.18) * entries
    return jnp.clip(entries, min=-most, max=most).astype(held_as)


def setup_inputs(seed: int = 0, part: int = 0) -> dict:
    key_list = jax.random.split(jax.random.key(seed), 7)
    part_keys = jax.random.split(jax.random.fold_in(key_list[6], part), 7)
    queries = draw_queries(jax.random.fold_in(jax.random.fold_in(key_list[6], part), 71), part)
    keys = draw_keys(jax.random.fold_in(jax.random.fold_in(key_list[6], part), 71), part)
    values = gaussian(part_keys[2], (TOKENS, HEAD_DIM), 1.0, 6.0, ((0, 64),))
    forward_out = gaussian(part_keys[3], (TOKENS, HEADS * HEAD_DIM), 1.0, 6.0, ((0, 64),))
    out_grad = gaussian(part_keys[4], (TOKENS, HEADS * HEAD_DIM), 4.0, 24.0, ((0, 64),))
    span_ids = draw_span_ids(jax.random.fold_in(jax.random.fold_in(key_list[6], part), 71), part)
    return dict(queries=queries, keys=keys, values=values, forward_out=forward_out, out_grad=out_grad, span_ids=span_ids)


NEG = -1.0e30


def reference(queries, keys, values, forward_out, out_grad, span_ids):
    offsets = jnp.arange(SPAN, dtype=jnp.int32)
    positions = (span_ids[:, None] * SPAN + offsets[None, :]).reshape(-1).astype(jnp.int32)
    visible = positions[None, :] <= positions[:, None]
    factor = 1.0 / (HEAD_DIM ** 0.5)

    def by_head(array):
        return array.reshape(TOKENS, HEADS, HEAD_DIM).transpose(1, 0, 2)

    def one_head(operands):
        q_rows, g_rows, o_rows = operands
        scores = jnp.dot(q_rows, keys.T, preferred_element_type=jnp.float32) * factor
        row_max = jnp.max(jnp.where(visible, scores, NEG), axis=1)
        shifted = jnp.where(visible, jnp.exp(scores - row_max[:, None]), 0.0)
        probs = shifted / jnp.sum(shifted, axis=1)[:, None]
        d_probs = jnp.dot(g_rows, values.T, preferred_element_type=jnp.float32)
        row_delta = jnp.sum(g_rows.astype(jnp.float32) * o_rows.astype(jnp.float32), axis=1)
        d_scores = (probs * (d_probs - row_delta[:, None])).astype(jnp.bfloat16)
        d_query = jnp.dot(d_scores, keys, preferred_element_type=jnp.float32) * factor
        d_key = jnp.dot(d_scores.T, q_rows, preferred_element_type=jnp.float32)
        d_value = jnp.dot(probs.astype(jnp.bfloat16).T, g_rows, preferred_element_type=jnp.float32)
        return d_query.astype(jnp.bfloat16), d_key, d_value

    d_query, d_key, d_value = lax.map(one_head, (by_head(queries), by_head(out_grad), by_head(forward_out)))
    d_queries = d_query.transpose(1, 0, 2).reshape(TOKENS, HEADS * HEAD_DIM)
    d_keys = jnp.zeros((TOKENS, HEAD_DIM), jnp.float32).at[positions].set(jnp.sum(d_key, axis=0) * factor)
    d_values = jnp.zeros((TOKENS, HEAD_DIM), jnp.float32).at[positions].set(jnp.sum(d_value, axis=0))
    return (d_queries, d_keys, d_values)
```

```python
import functools
import math

import jax
import jax.numpy as jnp
from jax import lax
from jax.experimental import pallas as pl
from jax.experimental.pallas import tpu as pltpu
from jax.sharding import PartitionSpec as P

NX, NZ, NY = 4, 8, 2
DEVICES = NX * NZ * NY
SPAN = 64
SPANS = 2 * DEVICES
WIDTH = 128
HEADS = 12
ROWS = HEADS * SPAN
KINDS = 2 * NY
COLS = KINDS * ROWS
KEYS = SPANS // NY * SPAN
TILE = 4 * SPAN
CHUNK = 256
BLOCK = 2 * SPAN + 16
FACTOR = 1.0 / math.sqrt(WIDTH)
SCALE = FACTOR * math.log2(math.e)
NEG = -1e30
VMEM_LIMIT = 24 * 1024 * 1024

F32 = jnp.float32
BF16 = jnp.bfloat16


def place(x, z, y):
    return ((x % NX) * NZ + z % NZ) * NY + y % NY


def shift(block, dx=0, dz=0, dy=0):
    pairs = [
        (place(x, z, y), place(x + dx, z + dz, y + dy))
        for x in range(NX)
        for z in range(NZ)
        for y in range(NY)
    ]
    return lax.ppermute(block, "ctx", pairs)


def spans_of(meta):
    low, other = (jnp.minimum(meta[i], SPANS - 1 - meta[i]) for i in range(2))
    first, second = jnp.minimum(low, other), jnp.maximum(low, other)
    spans = (first, second, SPANS - 1 - second, SPANS - 1 - first)
    return spans, jnp.where(low < other, 0, 1)


def pick(spans, kind):
    result = spans[0]
    for i in range(1, KINDS):
        result = jnp.where(kind == i, spans[i], result)
    return result


def columns(start, width=CHUNK):
    return pl.ds(pl.multiple_of(start, WIDTH), width)


def prepare_kernel(meta, q_own, g_own, o_own, q_other, g_other, qs, gs, qt, gt, delta, products):
    spans, mine = spans_of(meta)
    delta[...] = jnp.zeros((8, COLS), F32)
    for device, (q_ref, g_ref) in enumerate(((q_own, g_own), (q_other, g_other))):
        low_kind = mine if device == 0 else 1 - mine
        for slot in range(2):
            number = meta[device] if slot == 0 else SPANS - 1 - meta[device]
            kind = jnp.where(number < DEVICES, low_kind, KINDS - 1 - low_kind)
            base = kind * ROWS
            rows = slice(slot * SPAN, (slot + 1) * SPAN)
            for b in range(HEADS // 2):
                lanes = [slice(h * WIDTH, (h + 1) * WIDTH) for h in (2 * b, 2 * b + 1)]
                q = jnp.concatenate([q_ref[rows, i] for i in lanes], axis=0)
                g = jnp.concatenate([g_ref[rows, i] for i in lanes], axis=0)
                target = columns(base + b * WIDTH, WIDTH)
                qs[target, :] = q
                gs[target, :] = g
                qt[:, target] = q.T
                gt[:, target] = g.T
                if device == 0:
                    o = jnp.concatenate([o_own[rows, i] for i in lanes], axis=0)
                    total = jnp.sum((g.astype(F32) * o.astype(F32)).T, axis=0, keepdims=True)
                    delta[:, target] = jnp.broadcast_to(total, (8, WIDTH))


def sort_spans(parts, numbers_v, numbers_s, sem, sorted_ref):
    count = 0
    for part in parts:
        for b in range(part.shape[0] // BLOCK):
            tail = part[b * BLOCK + 2 * SPAN : (b + 1) * BLOCK, :WIDTH].astype(F32)
            tail = tail.astype(jnp.int32)
            numbers_v[count : count + 1, :] = tail[0:1, :]
            numbers_v[count + 1 : count + 2, :] = tail[8:9, :]
            count += 2
    copy = pltpu.make_async_copy(numbers_v, numbers_s, sem)
    copy.start()
    copy.wait()
    first = 0
    for part in parts:
        total = part.shape[0] // BLOCK

        def step(b, carry, part=part, first=first):
            start = pl.multiple_of(b * BLOCK, 16)
            for half in range(2):
                number = numbers_s[first + 2 * b + half, 0]
                target = pl.multiple_of(number // 2 * SPAN, SPAN)
                sorted_ref[pl.ds(target, SPAN), :] = part[pl.ds(start + half * SPAN, SPAN), :]
            return carry

        lax.fori_loop(0, total, step, 0, unroll=True)
        first += 2 * total


def hidden(tile, span, parity):
    index = lax.broadcasted_iota(jnp.int32, (TILE, CHUNK), 0)
    spans = (tile * (TILE // SPAN) + index // SPAN) * NY + parity - span
    key = spans * SPAN + index % SPAN
    row = lax.broadcasted_iota(jnp.int32, (TILE, CHUNK), 1) & (SPAN - 1)
    return key > row


def last_tile(span, parity):
    return jnp.maximum(span - parity, 0) // NY // (TILE // SPAN)


def key_rows(tile):
    return pl.ds(pl.multiple_of(tile * TILE, TILE), TILE)


def statistics_kernel(n_parts, meta, *refs):
    parts = refs[:n_parts]
    qt, delta, pairs, stats, numbers_v, numbers_s, sem = refs[n_parts:]
    sort_spans(parts, numbers_v, numbers_s, sem, pairs)
    spans, _ = spans_of(meta)
    parity = meta[4]
    for kind in range(KINDS):
        span = spans[kind]
        last = last_tile(span, parity)

        def visit(tile, state, masked, kind=kind, span=span):
            k = pairs[key_rows(tile), :WIDTH]
            fresh_state = []
            for c, (before, total) in enumerate(state):
                start = kind * ROWS + c * CHUNK
                s = jnp.dot(k, qt[:, start : start + CHUNK], preferred_element_type=F32) * SCALE
                if masked:
                    s = jnp.where(hidden(tile, span, parity), 2 * NEG, s)
                s = s.reshape(TILE // 8, 8, CHUNK)
                after = jnp.maximum(before, jnp.max(s, axis=0))
                fresh = jnp.sum(jnp.exp2(s - after[None]), axis=0)
                fresh_state.append((after, total * jnp.exp2(before - after) + fresh))
            return tuple(fresh_state)

        start = (jnp.full((8, CHUNK), NEG, F32), jnp.zeros((8, CHUNK), F32))
        state = (start,) * (ROWS // CHUNK)
        state = lax.fori_loop(0, last, lambda t, s: visit(t, s, False), state)
        state = visit(last, state, True)
        for c, (row_max, row_sum) in enumerate(state):
            cols = slice(kind * ROWS + c * CHUNK, kind * ROWS + (c + 1) * CHUNK)
            top = jnp.max(row_max, axis=0, keepdims=True)
            total = jnp.sum(row_sum * jnp.exp2(row_max - top), axis=0, keepdims=True)
            stats[0:1, cols] = top
            stats[1:2, cols] = total
            stats[2:3, cols] = delta[0:1, cols]
            stats[3:8, cols] = jnp.zeros((5, CHUNK), F32)


def gradients_kernel(meta, pairs, qs, gs, qt, gt, mine_ref, other_ref, *refs):
    dq_own, dq_other = refs[:2]
    out_refs = refs[2 : 2 + NX]
    level, delta, dqt, sums = refs[2 + NX :]
    spans, mine = spans_of(meta)
    my_x, my_z, parity = meta[2], meta[3], meta[4]
    top = jnp.maximum(mine_ref[0:1, :], other_ref[0:1, :])
    total = mine_ref[1:2, :] * jnp.exp2(mine_ref[0:1, :] - top)
    total += other_ref[1:2, :] * jnp.exp2(other_ref[0:1, :] - top)
    level[...] = top + jnp.log2(total)
    delta[...] = mine_ref[2:3, :] + other_ref[2:3, :]
    dqt[...] = jnp.zeros((WIDTH, COLS), F32)
    sums[...] = jnp.zeros((KEYS, 2 * WIDTH), F32)

    def kind_step(kind, carry):
        span = pick(spans, kind)
        last = last_tile(span, parity)

        def visit(tile, masked):
            rows = key_rows(tile)
            k = pairs[rows, :WIDTH]
            v = pairs[rows, WIDTH:]
            kt = k.T
            d_key = jnp.zeros((TILE, WIDTH), F32)
            d_value = jnp.zeros((TILE, WIDTH), F32)
            for c in range(ROWS // CHUNK):
                cols = columns(kind * ROWS + c * CHUNK)
                s = jnp.dot(k, qt[:, cols], preferred_element_type=F32) * SCALE
                p = jnp.exp2(s - level[:, cols])
                if masked:
                    p = jnp.where(hidden(tile, span, parity), 0.0, p)
                dp = jnp.dot(v, gt[:, cols], preferred_element_type=F32)
                ds = (p * (dp - delta[:, cols])).astype(BF16)
                d_value += jnp.dot(p.astype(BF16), gs[cols, :], preferred_element_type=F32)
                d_key += jnp.dot(ds, qs[cols, :], preferred_element_type=F32)
                dqt[:, cols] += jnp.dot(kt, ds, preferred_element_type=F32)
            sums[rows, :WIDTH] += d_key
            sums[rows, WIDTH:] += d_value

        lax.fori_loop(0, last, lambda t, c: visit(t, False), None)
        visit(last, True)
        return carry

    lax.fori_loop(0, KINDS, kind_step, 0)

    pair = 2 * SPAN
    for x_off in range(NX):
        x = (my_x + x_off) % NX
        for z_off in range(NZ):
            z = (my_z + z_off) % NZ
            source = pl.ds(pl.multiple_of((x * NZ + z) * pair, pair), pair)
            out_refs[x_off][z_off * pair : (z_off + 1) * pair, :] = sums[source, :].astype(BF16)
    for device, out in ((0, dq_own), (1, dq_other)):
        low_kind = mine if device == 0 else 1 - mine
        for slot in range(2):
            number = meta[device] if slot == 0 else SPANS - 1 - meta[device]
            kind = jnp.where(number < DEVICES, low_kind, KINDS - 1 - low_kind)
            for b in range(ROWS // WIDTH):
                block = dqt[:, columns(kind * ROWS + b * WIDTH, WIDTH)].T * FACTOR
                for half in range(2):
                    h = 2 * b + half
                    out[slot * SPAN : (slot + 1) * SPAN, h * WIDTH : (h + 1) * WIDTH] = block[
                        half * SPAN : (half + 1) * SPAN
                    ].astype(out.dtype)


def run(kernel, meta, arrays, outs, scratch, flops, name):
    return pl.pallas_call(
        kernel,
        out_shape=[jax.ShapeDtypeStruct(s, d) for s, d in outs],
        in_specs=[pl.BlockSpec(memory_space=pltpu.SMEM)]
        + [pl.BlockSpec(memory_space=pltpu.VMEM)] * len(arrays),
        out_specs=[pl.BlockSpec(memory_space=pltpu.VMEM)] * len(outs),
        scratch_shapes=scratch,
        compiler_params=pltpu.CompilerParams(vmem_limit_bytes=VMEM_LIMIT),
        cost_estimate=pl.CostEstimate(flops=flops, bytes_accessed=10**6, transcendentals=10**6),
        name=name,
    )(meta, *arrays)


def per_device(queries, keys, values, forward_out, out_grad, span_ids):
    me = lax.axis_index("ctx")
    my_x, my_z, my_y = me // (NZ * NY), (me // NY) % NZ, me % NY
    keep_first = (span_ids[0] & 1) == my_y
    kept_number = jnp.where(keep_first, span_ids[0], span_ids[1])
    sent_number = SPANS - 1 - kept_number
    both = jnp.concatenate([keys, values], axis=1)
    upper, lower = both[:SPAN], both[SPAN:]
    kept = jnp.where(keep_first, upper, lower)
    sent = jnp.where(keep_first, lower, upper)
    rows_of = lambda n, r: jnp.broadcast_to(n.astype(BF16), (r, 2 * WIDTH))
    sent = jnp.concatenate([sent, rows_of(sent_number, 8), rows_of(span_ids[0], 8)], axis=0)
    given = shift(sent, dy=1)
    other_first = given[SPAN + 8, 0].astype(jnp.int32)
    meta = jnp.stack([span_ids[0], other_first, my_x, my_z, my_y]).astype(jnp.int32)
    q_other = shift(queries, dy=1)
    g_other = shift(out_grad, dy=1)
    block = jnp.concatenate(
        [kept, given[:SPAN], rows_of(kept_number, 8), given[SPAN : SPAN + 8]], axis=0
    )
    ring = jnp.concatenate([block] + [shift(block, dz=d) for d in range(1, NZ)], axis=0)
    parts = [ring] + [shift(ring, dx=d) for d in range(1, NX)]

    wide = ((COLS, WIDTH), BF16)
    tall = ((WIDTH, COLS), BF16)
    flat = ((8, COLS), F32)
    qs, gs, qt, gt, delta = run(
        prepare_kernel,
        meta,
        [queries, out_grad, forward_out, q_other, g_other],
        [wide, wide, tall, tall, flat],
        [pltpu.VMEM((WIDTH, WIDTH), F32)],
        10**9,
        "prepare",
    )
    pairs, stats = run(
        functools.partial(statistics_kernel, NX),
        meta,
        parts + [qt, delta],
        [((KEYS, 2 * WIDTH), BF16), flat],
        [
            pltpu.VMEM((2 * NX * NZ, WIDTH), jnp.int32),
            pltpu.SMEM((2 * NX * NZ, WIDTH), jnp.int32),
            pltpu.SemaphoreType.DMA,
        ],
        2 * 10**9,
        "row_statistics",
    )
    other_stats = shift(stats, dy=1)
    dq_own, dq_sent, *grads = run(
        gradients_kernel,
        meta,
        [pairs, qs, gs, qt, gt, stats, other_stats],
        [((2 * SPAN, HEADS * WIDTH), F32), ((2 * SPAN, HEADS * WIDTH), BF16)]
        + [((KEYS // NX, 2 * WIDTH), BF16)] * NX,
        [
            pltpu.VMEM((1, COLS), F32),
            pltpu.VMEM((1, COLS), F32),
            pltpu.VMEM((WIDTH, COLS), F32),
            pltpu.VMEM((KEYS, 2 * WIDTH), F32),
        ],
        8 * 10**9,
        "gradients",
    )

    over_x = grads[0].astype(F32)
    for d in range(1, NX):
        over_x += shift(grads[d], dx=d).astype(F32)
    over_x = over_x.astype(BF16)
    pair = 2 * SPAN
    over_z = over_x[:pair].astype(F32)
    for d in range(1, NZ):
        over_z += shift(over_x[d * pair : (d + 1) * pair], dz=d).astype(F32)
    d_queries = (dq_own + shift(dq_sent, dy=1).astype(F32)).astype(BF16)
    first = my_y == 0
    upper, lower = over_z[:SPAN], over_z[SPAN:]
    given = shift(jnp.where(first, lower, upper), dy=1)
    final = jnp.where(
        first,
        jnp.concatenate([upper, given], axis=0),
        jnp.concatenate([given, lower], axis=0),
    )
    return (d_queries, final[:, :WIDTH] * FACTOR, final[:, WIDTH:])


def solution(mesh):
    rows = P(("dp", "ctx"), None)
    return jax.shard_map(
        per_device,
        mesh=mesh,
        in_specs=(rows, rows, rows, rows, rows, P(("dp", "ctx"))),
        out_specs=(rows, rows, rows),
        check_vma=False,
    )
```

```python
import functools
import math

import jax
import jax.numpy as jnp
from jax import lax
from jax.experimental import pallas as pl
from jax.experimental.pallas import tpu as pltpu
from jax.sharding import PartitionSpec as P

NX, NZ, NY = 4, 8, 2
DEVICES = NX * NZ * NY
SPAN = 64
SPANS = 2 * DEVICES
WIDTH = 128
HEADS = 12
ROWS = HEADS * SPAN
KINDS = 2 * NY
COLS = KINDS * ROWS
KEYS = SPANS // NY * SPAN
STATS_TILE = 8 * SPAN
TILE = 8 * SPAN
BLOCK = 2 * SPAN + 16
FACTOR = 1.0 / math.sqrt(WIDTH)
SCALE = FACTOR * math.log2(math.e)
NEG = -1e30
SAFE = 64.0
VMEM_LIMIT = 28 * 1024 * 1024

F32 = jnp.float32
BF16 = jnp.bfloat16


def place(x, z, y):
    return ((x % NX) * NZ + z % NZ) * NY + y % NY


def shift(block, dx=0, dz=0, dy=0):
    pairs = [
        (place(x, z, y), place(x + dx, z + dz, y + dy))
        for x in range(NX)
        for z in range(NZ)
        for y in range(NY)
    ]
    return lax.ppermute(block, "ctx", pairs)


def spans_of(meta):
    return meta[0], SPANS - 1 - meta[0], meta[1], SPANS - 1 - meta[1]


def pick(spans, kind):
    result = spans[0]
    for i in range(1, KINDS):
        result = jnp.where(kind == i, spans[i], result)
    return result


def columns(start, width=ROWS):
    return pl.ds(pl.multiple_of(start, WIDTH), width)


def numbers_rows(first, second):
    index = lax.broadcasted_iota(jnp.int32, (16, 2 * WIDTH), 0)
    return jnp.where(index < 8, first, second).astype(F32).astype(BF16)


def pack_kernel(ids, where, keys_any, values_any, kept, sent, keys, values, sem, sem_v):
    copies = [
        pltpu.make_async_copy(keys_any, keys, sem),
        pltpu.make_async_copy(values_any, values, sem_v),
    ]
    for copy in copies:
        copy.start()
    for copy in copies:
        copy.wait()
    keep = jnp.where((ids[0] & 1) == where[2], 0, 1)
    for target, slot in ((kept, keep), (sent, 1 - keep)):
        rows = pl.ds(pl.multiple_of(slot * SPAN, SPAN), SPAN)
        target[:SPAN, :WIDTH] = keys[rows, :]
        target[:SPAN, WIDTH:] = values[rows, :]
        number = jnp.where(slot == 0, ids[0], ids[1])
        target[SPAN:, :] = numbers_rows(number, ids[0])


def place_heads(own, refs, sources):
    for slot in range(2):
        rows = slice(slot * SPAN, (slot + 1) * SPAN)
        for b in range(HEADS // 2):
            lanes = [slice(h * WIDTH, (h + 1) * WIDTH) for h in (2 * b, 2 * b + 1)]
            start = ((0 if own else 2) + slot) * ROWS + b * WIDTH
            target = slice(start, start + WIDTH)
            blocks = []
            for source in sources:
                blocks.append(jnp.concatenate([source[rows, i] for i in lanes], axis=0))
            for (tall, wide), block in zip(refs, blocks):
                wide[target, :] = block
                tall[:, target] = block.T
            if own:
                yield target, blocks


def own_rows_kernel(q_own, g_own, o_own, qs, gs, qt, gt, delta):
    for target, (_, g, o) in place_heads(True, ((qt, qs), (gt, gs)), (q_own, g_own, o_own)):
        total = jnp.sum((g.astype(F32) * o.astype(F32)).T, axis=0, keepdims=True)
        delta[:, target] = jnp.broadcast_to(total, (8, WIDTH))


def other_rows_kernel(q_other, g_other, *refs):
    qs, gs, qt, gt = refs[4:]
    for _ in place_heads(False, ((qt, qs), (gt, gs)), (q_other, g_other)):
        pass


def read_numbers(parts):
    found = []
    for part in parts:
        for b in range(part.shape[0] // BLOCK):
            tail = part[b * BLOCK + 2 * SPAN : (b + 1) * BLOCK, :WIDTH].astype(F32)
            for half in range(2):
                found.append((tail[8 * half, 0].astype(jnp.int32), part, b * BLOCK + half * SPAN))
    return found


def sort_kernel(n_parts, *refs):
    parts, (pairs, sums, dqt) = refs[:n_parts], refs[n_parts:]
    sums[...] = jnp.zeros(sums.shape, F32)
    dqt[...] = jnp.zeros(dqt.shape, F32)
    for number, part, row in read_numbers(parts):
        target = pl.multiple_of(number // NY * SPAN, SPAN)
        pairs[pl.ds(target, SPAN), :] = part[row : row + SPAN, :]


def hidden(offsets, shape):
    index = lax.broadcasted_iota(jnp.int32, shape, 0)
    offset = offsets[0]
    for i in range(1, len(offsets)):
        offset = jnp.where(index >= i * SPAN, offsets[i], offset)
    row = lax.broadcasted_iota(jnp.int32, shape, 1) & (SPAN - 1)
    return offset * SPAN + (index & (SPAN - 1)) > row


def statistics_kernel(n_parts, first, last, meta, *refs):
    parts, refs = refs[:n_parts], list(refs[n_parts:])
    qt = refs.pop(0)
    before_ref = None if first else refs.pop(0)
    delta = refs.pop(0) if last else None
    out, row_max, row_sum, base, top, extra, keys, ordered = refs
    spans = spans_of(meta)
    found = read_numbers(parts)
    for number, part, row in found:
        rank = sum((other < number).astype(jnp.int32) for other, _, _ in found)
        ordered[rank] = number
        target = pl.multiple_of(rank * SPAN, SPAN)
        keys[pl.ds(target, SPAN), :] = part[row : row + SPAN, :WIDTH]
    if first:
        row_max[...] = jnp.full((8, COLS), NEG, F32)
        row_sum[...] = jnp.zeros((8, COLS), F32)
    else:
        row_max[...] = before_ref[:8, :]
        row_sum[...] = before_ref[8:, :]
    group = STATS_TILE // SPAN

    def visit_all(visit):
        def step(kind, carry):
            span = pick(spans, kind)
            cols = columns(kind * ROWS)

            def scores(tile, masked):
                k = keys[pl.ds(pl.multiple_of(tile * STATS_TILE, STATS_TILE), STATS_TILE), :]
                s = jnp.dot(k, qt[:, cols], preferred_element_type=F32) * SCALE
                if masked:
                    offsets = [ordered[tile * group + i] - span for i in range(group)]
                    s = jnp.where(hidden(offsets, s.shape), 2 * NEG, s)
                visit(s.reshape(STATS_TILE // 8, 8, ROWS), cols)

            full = sum((number < span).astype(jnp.int32) for number, _, _ in found) // group
            seen = sum((number <= span).astype(jnp.int32) for number, _, _ in found)
            lax.fori_loop(0, full, lambda t, c: scores(t, False), None)

            @pl.when(seen > full * group)
            def _():
                scores(full, True)

            return carry

        lax.fori_loop(0, KINDS, step, 0)

    def against_base(s, cols):
        top[:, cols] = jnp.maximum(top[:, cols], jnp.max(s, axis=0))
        extra[:, cols] += jnp.sum(jnp.exp2(s - base[:, cols][None]), axis=0)

    def against_maximum(s, cols):
        before = row_max[:, cols]
        after = jnp.maximum(before, jnp.max(s, axis=0))
        fresh = jnp.sum(jnp.exp2(s - after[None]), axis=0)
        row_sum[:, cols] = row_sum[:, cols] * jnp.exp2(before - after) + fresh
        row_max[:, cols] = after

    unset = row_max[...] <= NEG
    base[...] = jnp.where(unset, 0.0, row_max[...])
    top[...] = jnp.full((8, COLS), 2 * NEG, F32)
    extra[...] = jnp.zeros((8, COLS), F32)
    visit_all(against_base)
    unset = row_max[...] <= NEG
    seen = top[...] > NEG
    gap = top[...] - base[...]
    far = seen & ((gap > SAFE) | (unset & (gap < -SAFE)))
    any_far = jnp.max(jnp.where(far, 1.0, 0.0)) > 0.0

    @pl.when(jnp.logical_not(any_far))
    def _():
        empty = unset & jnp.logical_not(seen)
        after = jnp.maximum(base[...], top[...])
        total = (row_sum[...] + extra[...]) * jnp.exp2(base[...] - after)
        row_sum[...] = jnp.where(empty, 0.0, total)
        row_max[...] = jnp.where(empty, NEG, after)

    @pl.when(any_far)
    def _():
        visit_all(against_maximum)

    if not last:
        out[:8, :] = row_max[...]
        out[8:, :] = row_sum[...]
    else:
        most = jnp.max(row_max[...], axis=0, keepdims=True)
        total = jnp.sum(row_sum[...] * jnp.exp2(row_max[...] - most), axis=0, keepdims=True)
        out[0:1, :] = most
        out[1:2, :] = total
        out[2:3, : 2 * ROWS] = delta[0:1, :]
        out[2:3, 2 * ROWS :] = jnp.zeros((1, 2 * ROWS), F32)
        out[3:8, :] = jnp.zeros((5, COLS), F32)


ORDER = (2, 1, NX - 1, 0)
TILES = KEYS // NX // TILE
STAGES = ((0,), (1, 2), (3,))


def gradients_kernel(stage, meta, pairs, qs, gs, qt, gt, mine_ref, other_ref, _sums, _dqt, *refs):
    sums, dqt = refs[:2]
    outs, (level, delta) = refs[2:-2], refs[-2:]
    spans = spans_of(meta)
    my_x, my_z, parity = meta[2], meta[3], meta[4]
    half = 2 * ROWS
    for mine, other in ((slice(0, half), slice(half, COLS)), (slice(half, COLS), slice(0, half))):
        top = jnp.maximum(mine_ref[0:1, mine], other_ref[0:1, other])
        total = mine_ref[1:2, mine] * jnp.exp2(mine_ref[0:1, mine] - top)
        total += other_ref[1:2, other] * jnp.exp2(other_ref[0:1, other] - top)
        level[:, mine] = top + jnp.log2(total)
        delta[:, mine] = mine_ref[2:3, mine] + other_ref[2:3, other]
    group = TILE // SPAN
    lasts = [jnp.maximum(span - parity, 0) // NY // group for span in spans]
    firsts = [(my_x + off) % NX * TILES for off in ORDER]
    counts = [
        sum(jnp.clip(last - first + 1, 0, TILES) for last in lasts) for first in firsts
    ]
    ready = [sum(counts[: entries[-1] + 1]) for entries in STAGES]
    everything = ready[-1]
    ends = [
        jnp.maximum(needed, (everything * (i + 1) + len(STAGES) - 1) // len(STAGES))
        for i, needed in enumerate(ready)
    ]
    begin = 0 if stage == 0 else ends[stage - 1]
    end = ends[stage]

    def visit(kind, tile, masked):
        span = pick(spans, kind)
        cols = columns(kind * ROWS)
        rows = pl.ds(pl.multiple_of(tile * TILE, TILE), TILE)
        k = pairs[rows, :WIDTH]
        v = pairs[rows, WIDTH:]
        s = jnp.dot(k, qt[:, cols], preferred_element_type=F32) * SCALE
        p = jnp.exp2(s - level[:, cols])
        if masked:
            offsets = [(tile * group + j) * NY + parity - span for j in range(group)]
            p = jnp.where(hidden(offsets, p.shape), 0.0, p)
        dp = jnp.dot(v, gt[:, cols], preferred_element_type=F32)
        ds = (p * (dp - delta[:, cols])).astype(BF16)
        d_value = jnp.dot(p.astype(BF16), gs[cols, :], preferred_element_type=F32)
        d_key = jnp.dot(ds, qs[cols, :], preferred_element_type=F32)
        dqt[:, cols] += jnp.dot(k.T, ds, preferred_element_type=F32)
        sums[rows, :WIDTH] += d_key
        sums[rows, WIDTH:] += d_value

    def step(i, done):
        entry, kind, part = i // (KINDS * TILES), i // TILES % KINDS, i % TILES
        tile = pick(firsts, entry) + part
        last = pick(lasts, kind)
        active = tile <= last
        now = active & (done >= begin) & (done < end)

        @pl.when(now & (tile < last))
        def _():
            visit(kind, tile, False)

        @pl.when(now & (tile == last))
        def _():
            visit(kind, tile, True)

        return done + active.astype(jnp.int32)

    lax.fori_loop(0, len(ORDER) * KINDS * TILES, step, jnp.int32(0))
    pair = 2 * SPAN
    for entry, out in zip(STAGES[stage], outs):
        for z_off in range(NZ):
            start = firsts[entry] * TILE + (my_z + z_off) % NZ * pair
            source = pl.ds(pl.multiple_of(start, pair), pair)
            out[z_off * pair : (z_off + 1) * pair, :] = sums[source, :].astype(out.dtype)


def d_queries_kernel(dqt, dq_own, dq_other):
    for device, out in enumerate((dq_own, dq_other)):
        for slot in range(2):
            for b in range(ROWS // WIDTH):
                start = (2 * device + slot) * ROWS + b * WIDTH
                block = dqt[:, start : start + WIDTH].T * FACTOR
                for half in range(2):
                    h = 2 * b + half
                    out[slot * SPAN : (slot + 1) * SPAN, h * WIDTH : (h + 1) * WIDTH] = block[
                        half * SPAN : (half + 1) * SPAN
                    ].astype(out.dtype)


def run(kernel, scalars, arrays, outs, scratch, flops, name, far=(), aliases=None):
    spaces = [pltpu.SMEM] * len(scalars)
    spaces += [pltpu.HBM if i in far else pltpu.VMEM for i in range(len(arrays))]
    return pl.pallas_call(
        kernel,
        out_shape=[jax.ShapeDtypeStruct(s, d) for s, d in outs],
        in_specs=[pl.BlockSpec(memory_space=space) for space in spaces],
        out_specs=[pl.BlockSpec(memory_space=pltpu.VMEM)] * len(outs),
        scratch_shapes=scratch,
        input_output_aliases=aliases or {},
        compiler_params=pltpu.CompilerParams(vmem_limit_bytes=VMEM_LIMIT),
        cost_estimate=pl.CostEstimate(flops=flops, bytes_accessed=10**5, transcendentals=0),
        name=name,
    )(*scalars, *arrays)


WIDE = ((COLS, WIDTH), BF16)
TALL = ((WIDTH, COLS), BF16)
FLAT = ((8, COLS), F32)
OWN = (2 * SPAN, HEADS * WIDTH)
SUMS = ((KEYS, 2 * WIDTH), F32)
DQT = ((WIDTH, COLS), F32)


def statistics(meta, parts, qt, before, delta):
    first, last = before is None, delta is not None
    count = sum(part.shape[0] // BLOCK * 2 for part in parts)
    arrays = list(parts) + [qt] + [a for a in (before, delta) if a is not None]
    return run(
        functools.partial(statistics_kernel, len(parts), first, last),
        [meta],
        arrays,
        [FLAT if last else ((16, COLS), F32)],
        [pltpu.VMEM((8, COLS), F32)] * 5
        + [pltpu.VMEM((count * SPAN, WIDTH), BF16), pltpu.SMEM((count,), jnp.int32)],
        2 * 10**9,
        "row_statistics",
    )[0]


def gradients(stage, meta, arrays, state, dtype):
    share = ((KEYS // NX, 2 * WIDTH), dtype)
    count = 1 + len(arrays)
    return run(
        functools.partial(gradients_kernel, stage),
        [meta],
        arrays + list(state),
        [SUMS, DQT] + [share] * len(STAGES[stage]),
        [pltpu.VMEM((1, COLS), F32)] * 2,
        8 * 10**9,
        "gradients",
        aliases={count: 0, count + 1: 1},
    )


def per_device(queries, keys, values, forward_out, out_grad, span_ids):
    me = lax.axis_index("ctx")
    my_x, my_z, my_y = me // (NZ * NY), (me // NY) % NZ, me % NY
    where = jnp.stack([my_x, my_z, my_y]).astype(jnp.int32)
    carried = ((SPAN + 16, 2 * WIDTH), BF16)
    sem = pltpu.SemaphoreType.DMA
    local = pltpu.VMEM((2 * SPAN, WIDTH), BF16)
    kept, sent = run(
        pack_kernel, [span_ids, where], [keys, values], [carried] * 2, [local, local, sem, sem],
        10, "pack", far=(0, 1),
    )
    given = shift(sent, dy=1)
    qs, gs, qt, gt, delta = run(
        own_rows_kernel, [], [queries, out_grad, forward_out],
        [WIDE, WIDE, TALL, TALL, ((8, COLS // 2), F32)], [], 10**9, "own_rows",
    )
    other_first = given[SPAN + 8, 0].astype(jnp.int32)
    meta = jnp.concatenate([span_ids[:1], other_first[None], where])
    block = jnp.concatenate(
        [kept[:SPAN], given[:SPAN], kept[SPAN : SPAN + 8], given[SPAN : SPAN + 8]], axis=0
    )
    q_other = shift(queries, dy=1)
    g_other = shift(out_grad, dy=1)

    ring = jnp.concatenate([block] + [shift(block, dx=d) for d in range(1, NX)], axis=0)
    ring, q_other, qs, gs, qt, gt, delta = lax.optimization_barrier(
        (ring, q_other, qs, gs, qt, gt, delta)
    )

    qs, gs, qt, gt = run(
        other_rows_kernel, [], [q_other, g_other, qs, gs, qt, gt], [WIDE, WIDE, TALL, TALL], [],
        10**9, "other_rows", aliases={2: 0, 3: 1, 4: 2, 5: 3},
    )
    half = ring.shape[0] // 2
    gathered = [ring]
    arrived, stats = (ring,), None
    for i in range(NZ // 2):
        up, down = arrived[0], arrived[-1]
        if i == NZ // 2 - 1:
            up, down = up[:half], down[half:]
        up, down = shift(up, dz=1), shift(down, dz=-1)
        stats = statistics(meta, arrived, qt, stats, None)
        up, down, stats, delta = lax.optimization_barrier((up, down, stats, delta))
        arrived = (up, down)
        gathered += arrived
    stats = statistics(meta, arrived, qt, stats, delta)
    other_stats = shift(stats, dy=1)
    pairs, *state = run(
        functools.partial(sort_kernel, len(gathered)), [], gathered,
        [((KEYS, 2 * WIDTH), BF16), SUMS, DQT], [], 10**9, "sort",
    )

    arrays = [pairs, qs, gs, qt, gt, stats, other_stats]
    *state, far = gradients(0, meta, arrays, state, BF16)
    far = shift(far, dx=ORDER[0])
    *state, up, down = gradients(1, meta, arrays, state, BF16)
    up, down = shift(up, dx=1), shift(down, dx=-1)
    far, *state = lax.optimization_barrier((far, *state))
    *state, own = gradients(2, meta, arrays, state, F32)
    dqt = state[1]
    over_x = [own, far, up, down]
    dq_own, dq_sent = run(
        d_queries_kernel, [], [dqt], [(OWN, F32), (OWN, BF16)], [], 10**8, "d_queries"
    )

    over_x = sum(part.astype(F32) for part in over_x).astype(BF16)
    over_x, dq_own, dq_sent = lax.optimization_barrier((over_x, dq_own, dq_sent))
    pair = 2 * SPAN
    over_z = over_x[:pair].astype(F32)
    for d in range(1, NZ):
        over_z += shift(over_x[d * pair : (d + 1) * pair], dz=d).astype(F32)
    dq_given = shift(dq_sent, dy=1)
    over_z, dq_given = lax.optimization_barrier((over_z, dq_given))
    d_queries = (dq_own + dq_given.astype(F32)).astype(BF16)
    first = my_y == 0
    upper, lower = over_z[:SPAN], over_z[SPAN:]
    given = shift(jnp.where(first, lower, upper), dy=1)
    final = jnp.where(
        first,
        jnp.concatenate([upper, given], axis=0),
        jnp.concatenate([given, lower], axis=0),
    )
    return (d_queries, final[:, :WIDTH] * FACTOR, final[:, WIDTH:])


def solution(mesh):
    rows = P(("dp", "ctx"), None)
    return jax.shard_map(
        per_device,
        mesh=mesh,
        in_specs=(rows, rows, rows, rows, rows, P(("dp", "ctx"))),
        out_specs=(rows, rows, rows),
        check_vma=False,
    )
```

```python
import functools
import math

import jax
import jax.numpy as jnp
from jax import lax
from jax.experimental import pallas as pl
from jax.experimental.pallas import tpu as pltpu
from jax.sharding import PartitionSpec as P

NX, NZ, NY = 4, 8, 2
DEVICES = NX * NZ * NY
SPAN = 64
SPANS = 2 * DEVICES
WIDTH = 128
HEADS = 12
ROWS = HEADS * SPAN
KINDS = 2 * NY
COLS = KINDS * ROWS
KEYS = SPANS // NY * SPAN
STATS_TILE = 8 * SPAN
TILE = 8 * SPAN
BLOCK = 2 * SPAN + 16
FACTOR = 1.0 / math.sqrt(WIDTH)
SCALE = FACTOR * math.log2(math.e)
NEG = -1e30
SAFE = 64.0
VMEM_LIMIT = 28 * 1024 * 1024

F32 = jnp.float32
BF16 = jnp.bfloat16


def place(x, z, y):
    return ((x % NX) * NZ + z % NZ) * NY + y % NY


def shift(block, dx=0, dz=0, dy=0):
    pairs = [
        (place(x, z, y), place(x + dx, z + dz, y + dy))
        for x in range(NX)
        for z in range(NZ)
        for y in range(NY)
    ]
    return lax.ppermute(block, "ctx", pairs)


def spans_of(meta):
    return meta[0], SPANS - 1 - meta[0], meta[1], SPANS - 1 - meta[1]


def pick(spans, kind):
    result = spans[0]
    for i in range(1, KINDS):
        result = jnp.where(kind == i, spans[i], result)
    return result


def columns(start, width=ROWS):
    return pl.ds(pl.multiple_of(start, WIDTH), width)


def numbers_rows(first, second):
    index = lax.broadcasted_iota(jnp.int32, (16, 2 * WIDTH), 0)
    return jnp.where(index < 8, first, second).astype(F32).astype(BF16)


def pack_kernel(ids, where, keys_any, values_any, kept, sent, keys, values, sem, sem_v):
    copies = [
        pltpu.make_async_copy(keys_any, keys, sem),
        pltpu.make_async_copy(values_any, values, sem_v),
    ]
    for copy in copies:
        copy.start()
    for copy in copies:
        copy.wait()
    keep = jnp.where((ids[0] & 1) == where[2], 0, 1)
    for target, slot in ((kept, keep), (sent, 1 - keep)):
        rows = pl.ds(pl.multiple_of(slot * SPAN, SPAN), SPAN)
        target[:SPAN, :WIDTH] = keys[rows, :]
        target[:SPAN, WIDTH:] = values[rows, :]
        number = jnp.where(slot == 0, ids[0], ids[1])
        target[SPAN:, :] = numbers_rows(number, ids[0])


def join_kernel(ids, where, kept, given, block, meta):
    block[:SPAN, :] = kept[:SPAN, :]
    block[SPAN : 2 * SPAN, :] = given[:SPAN, :]
    mine, other = kept[SPAN:, :].astype(F32), given[SPAN:, :].astype(F32)
    block[2 * SPAN :, :] = jnp.concatenate([mine[:8], other[:8]], axis=0).astype(BF16)
    meta[0] = ids[0]
    meta[1] = other[8, 0].astype(jnp.int32)
    for i in range(3):
        meta[2 + i] = where[i]


def place_heads(own, refs, sources):
    for slot in range(2):
        rows = slice(slot * SPAN, (slot + 1) * SPAN)
        for b in range(HEADS // 2):
            lanes = [slice(h * WIDTH, (h + 1) * WIDTH) for h in (2 * b, 2 * b + 1)]
            start = ((0 if own else 2) + slot) * ROWS + b * WIDTH
            target = slice(start, start + WIDTH)
            blocks = []
            for source in sources:
                blocks.append(jnp.concatenate([source[rows, i] for i in lanes], axis=0))
            for (tall, wide), block in zip(refs, blocks):
                wide[target, :] = block
                tall[:, target] = block.T
            if own:
                yield target, blocks


def own_rows_kernel(q_own, g_own, o_own, qs, gs, qt, gt, delta):
    for target, (_, g, o) in place_heads(True, ((qt, qs), (gt, gs)), (q_own, g_own, o_own)):
        total = jnp.sum((g.astype(F32) * o.astype(F32)).T, axis=0, keepdims=True)
        delta[:, target] = jnp.broadcast_to(total, (8, WIDTH))


def other_rows_kernel(rows, _wide, _tall, wide, tall):
    for _ in place_heads(False, ((tall, wide),), (rows,)):
        pass


def read_numbers(parts):
    found = []
    for part in parts:
        for b in range(part.shape[0] // BLOCK):
            tail = part[b * BLOCK + 2 * SPAN : (b + 1) * BLOCK, :WIDTH].astype(F32)
            for half in range(2):
                found.append((tail[8 * half, 0].astype(jnp.int32), part, b * BLOCK + half * SPAN))
    return found


def sort_kernel(n_parts, *refs):
    parts, (pairs, sums, dqt) = refs[:n_parts], refs[n_parts:]
    sums[...] = jnp.zeros(sums.shape, F32)
    dqt[...] = jnp.zeros(dqt.shape, F32)
    for number, part, row in read_numbers(parts):
        target = pl.multiple_of(number // NY * SPAN, SPAN)
        pairs[pl.ds(target, SPAN), :] = part[row : row + SPAN, :]


def hidden(offsets, shape):
    index = lax.broadcasted_iota(jnp.int32, shape, 0)
    offset = offsets[0]
    for i in range(1, len(offsets)):
        offset = jnp.where(index >= i * SPAN, offsets[i], offset)
    row = lax.broadcasted_iota(jnp.int32, shape, 1) & (SPAN - 1)
    return offset * SPAN + (index & (SPAN - 1)) > row


def statistics_kernel(n_parts, first, last, meta, *refs):
    parts, refs = refs[:n_parts], list(refs[n_parts:])
    qt = refs.pop(0)
    before_ref = None if first else refs.pop(0)
    delta = refs.pop(0) if last else None
    out, row_max, row_sum, base, top, extra, keys, ordered = refs
    spans = spans_of(meta)
    found = read_numbers(parts)
    for number, part, row in found:
        rank = sum((other < number).astype(jnp.int32) for other, _, _ in found)
        ordered[rank] = number
        target = pl.multiple_of(rank * SPAN, SPAN)
        keys[pl.ds(target, SPAN), :] = part[row : row + SPAN, :WIDTH]
    if first:
        row_max[...] = jnp.full((8, COLS), NEG, F32)
        row_sum[...] = jnp.zeros((8, COLS), F32)
    else:
        row_max[...] = before_ref[:8, :]
        row_sum[...] = before_ref[8:, :]
    group = STATS_TILE // SPAN

    def visit_all(visit, width, always_masked):
        def step(i, carry):
            kind = i // (ROWS // width)
            span = pick(spans, kind)
            cols = columns(i * width, width)

            def scores(tile, masked):
                k = keys[pl.ds(pl.multiple_of(tile * STATS_TILE, STATS_TILE), STATS_TILE), :]
                s = jnp.dot(k, qt[:, cols], preferred_element_type=F32) * SCALE
                if masked:
                    offsets = [ordered[tile * group + i] - span for i in range(group)]
                    s = jnp.where(hidden(offsets, s.shape), 2 * NEG, s)
                visit(s.reshape(STATS_TILE // 8, 8, width), cols)

            full = sum((number < span).astype(jnp.int32) for number, _, _ in found) // group
            seen = sum((number <= span).astype(jnp.int32) for number, _, _ in found)
            if always_masked:
                tiles = (seen + group - 1) // group
                lax.fori_loop(0, tiles, lambda t, c: scores(t, True), None)
                return carry
            lax.fori_loop(0, full, lambda t, c: scores(t, False), None)

            @pl.when(seen > full * group)
            def _():
                scores(full, True)

            return carry

        lax.fori_loop(0, COLS // width, step, 0)

    def against_base(s, cols):
        top[:, cols] = jnp.maximum(top[:, cols], jnp.max(s, axis=0))
        extra[:, cols] += jnp.sum(jnp.exp2(s - base[:, cols][None]), axis=0)

    def against_maximum(s, cols):
        before = row_max[:, cols]
        after = jnp.maximum(before, jnp.max(s, axis=0))
        fresh = jnp.sum(jnp.exp2(s - after[None]), axis=0)
        row_sum[:, cols] = row_sum[:, cols] * jnp.exp2(before - after) + fresh
        row_max[:, cols] = after

    unset = row_max[...] <= NEG
    base[...] = jnp.where(unset, 0.0, row_max[...])
    top[...] = jnp.full((8, COLS), 2 * NEG, F32)
    extra[...] = jnp.zeros((8, COLS), F32)
    visit_all(against_base, ROWS, False)
    unset = row_max[...] <= NEG
    seen = top[...] > NEG
    gap = top[...] - base[...]
    far = seen & ((gap > SAFE) | (unset & (gap < -SAFE)))
    any_far = jnp.max(jnp.where(far, 1.0, 0.0)) > 0.0

    @pl.when(jnp.logical_not(any_far))
    def _():
        empty = unset & jnp.logical_not(seen)
        after = jnp.maximum(base[...], top[...])
        total = (row_sum[...] + extra[...]) * jnp.exp2(base[...] - after)
        row_sum[...] = jnp.where(empty, 0.0, total)
        row_max[...] = jnp.where(empty, NEG, after)

    @pl.when(any_far)
    def _():
        visit_all(against_maximum, WIDTH, True)

    if not last:
        out[:8, :] = row_max[...]
        out[8:, :] = row_sum[...]
    else:
        most = jnp.max(row_max[...], axis=0, keepdims=True)
        total = jnp.sum(row_sum[...] * jnp.exp2(row_max[...] - most), axis=0, keepdims=True)
        out[0:1, :] = most
        out[1:2, :] = total
        out[2:3, : 2 * ROWS] = delta[0:1, :]
        out[2:3, 2 * ROWS :] = jnp.zeros((1, 2 * ROWS), F32)
        out[3:8, :] = jnp.zeros((5, COLS), F32)


ORDER = (2, 1, NX - 1, 0)
TILES = KEYS // NX // TILE
STAGES = ((0,), (1, 2), (3,))


def gradients_kernel(stage, meta, pairs, qs, gs, qt, gt, mine_ref, other_ref, _sums, _dqt, *refs):
    sums, dqt = refs[:2]
    outs, (level, delta) = refs[2:-2], refs[-2:]
    spans = spans_of(meta)
    my_x, my_z, parity = meta[2], meta[3], meta[4]
    half = 2 * ROWS
    for mine, other in ((slice(0, half), slice(half, COLS)), (slice(half, COLS), slice(0, half))):
        top = jnp.maximum(mine_ref[0:1, mine], other_ref[0:1, other])
        total = mine_ref[1:2, mine] * jnp.exp2(mine_ref[0:1, mine] - top)
        total += other_ref[1:2, other] * jnp.exp2(other_ref[0:1, other] - top)
        level[:, mine] = top + jnp.log2(total)
        delta[:, mine] = mine_ref[2:3, mine] + other_ref[2:3, other]
    group = TILE // SPAN
    lasts = [jnp.maximum(span - parity, 0) // NY // group for span in spans]
    firsts = [(my_x + off) % NX * TILES for off in ORDER]
    counts = [
        sum(jnp.clip(last - first + 1, 0, TILES) for last in lasts) for first in firsts
    ]
    ready = [sum(counts[: entries[-1] + 1]) for entries in STAGES]
    everything = ready[-1]
    ends = [
        jnp.maximum(needed, (everything * (i + 1) + len(STAGES) - 1) // len(STAGES))
        for i, needed in enumerate(ready)
    ]
    begin = 0 if stage == 0 else ends[stage - 1]
    end = ends[stage]

    def visit(kind, tile, masked):
        span = pick(spans, kind)
        cols = columns(kind * ROWS)
        rows = pl.ds(pl.multiple_of(tile * TILE, TILE), TILE)
        k = pairs[rows, :WIDTH]
        v = pairs[rows, WIDTH:]
        s = jnp.dot(k, qt[:, cols], preferred_element_type=F32) * SCALE
        p = jnp.exp2(s - level[:, cols])
        if masked:
            offsets = [(tile * group + j) * NY + parity - span for j in range(group)]
            p = jnp.where(hidden(offsets, p.shape), 0.0, p)
        dp = jnp.dot(v, gt[:, cols], preferred_element_type=F32)
        ds = (p * (dp - delta[:, cols])).astype(BF16)
        d_value = jnp.dot(p.astype(BF16), gs[cols, :], preferred_element_type=F32)
        d_key = jnp.dot(ds, qs[cols, :], preferred_element_type=F32)
        dqt[:, cols] += jnp.dot(k.T, ds, preferred_element_type=F32)
        sums[rows, :WIDTH] += d_key
        sums[rows, WIDTH:] += d_value

    def step(i, done):
        entry, kind, part = i // (KINDS * TILES), i // TILES % KINDS, i % TILES
        tile = pick(firsts, entry) + part
        last = pick(lasts, kind)
        active = tile <= last
        now = active & (done >= begin) & (done < end)

        @pl.when(now & (tile < last))
        def _():
            visit(kind, tile, False)

        @pl.when(now & (tile == last))
        def _():
            visit(kind, tile, True)

        return done + active.astype(jnp.int32)

    lax.fori_loop(0, len(ORDER) * KINDS * TILES, step, jnp.int32(0))
    pair = 2 * SPAN
    for entry, out in zip(STAGES[stage], outs):
        for z_off in range(NZ):
            start = firsts[entry] * TILE + (my_z + z_off) % NZ * pair
            source = pl.ds(pl.multiple_of(start, pair), pair)
            out[z_off * pair : (z_off + 1) * pair, :] = sums[source, :].astype(out.dtype)


def d_queries_kernel(dqt, dq_own, dq_other):
    for device, out in enumerate((dq_own, dq_other)):
        for slot in range(2):
            for b in range(ROWS // WIDTH):
                start = (2 * device + slot) * ROWS + b * WIDTH
                block = dqt[:, start : start + WIDTH].T * FACTOR
                for half in range(2):
                    h = 2 * b + half
                    out[slot * SPAN : (slot + 1) * SPAN, h * WIDTH : (h + 1) * WIDTH] = block[
                        half * SPAN : (half + 1) * SPAN
                    ].astype(out.dtype)


def run(kernel, scalars, arrays, outs, scratch, flops, name, far=(), aliases=None, scalar_outs=()):
    spaces = [pltpu.SMEM] * len(scalars)
    spaces += [pltpu.HBM if i in far else pltpu.VMEM for i in range(len(arrays))]
    return pl.pallas_call(
        kernel,
        out_shape=[jax.ShapeDtypeStruct(s, d) for s, d in outs],
        in_specs=[pl.BlockSpec(memory_space=space) for space in spaces],
        out_specs=[
            pl.BlockSpec(memory_space=pltpu.SMEM if i in scalar_outs else pltpu.VMEM)
            for i in range(len(outs))
        ],
        scratch_shapes=scratch,
        input_output_aliases=aliases or {},
        compiler_params=pltpu.CompilerParams(vmem_limit_bytes=VMEM_LIMIT),
        cost_estimate=pl.CostEstimate(flops=flops, bytes_accessed=10**5, transcendentals=0),
        name=name,
    )(*scalars, *arrays)


WIDE = ((COLS, WIDTH), BF16)
TALL = ((WIDTH, COLS), BF16)
FLAT = ((8, COLS), F32)
OWN = (2 * SPAN, HEADS * WIDTH)
SUMS = ((KEYS, 2 * WIDTH), F32)
DQT = ((WIDTH, COLS), F32)


def statistics(meta, parts, qt, before, delta):
    first, last = before is None, delta is not None
    count = sum(part.shape[0] // BLOCK * 2 for part in parts)
    arrays = list(parts) + [qt] + [a for a in (before, delta) if a is not None]
    return run(
        functools.partial(statistics_kernel, len(parts), first, last),
        [meta],
        arrays,
        [FLAT if last else ((16, COLS), F32)],
        [pltpu.VMEM((8, COLS), F32)] * 5
        + [pltpu.VMEM((count * SPAN, WIDTH), BF16), pltpu.SMEM((count,), jnp.int32)],
        2 * 10**9,
        "row_statistics",
    )[0]


def other_rows(rows, wide, tall):
    return run(
        other_rows_kernel, [], [rows, wide, tall], [WIDE, TALL], [], 10**9, "other_rows",
        aliases={1: 0, 2: 1},
    )


def gradients(stage, meta, arrays, state, dtype):
    share = ((KEYS // NX, 2 * WIDTH), dtype)
    count = 1 + len(arrays)
    return run(
        functools.partial(gradients_kernel, stage),
        [meta],
        arrays + list(state),
        [SUMS, DQT] + [share] * len(STAGES[stage]),
        [pltpu.VMEM((1, COLS), F32)] * 2,
        8 * 10**9,
        "gradients",
        aliases={count: 0, count + 1: 1},
    )


def per_device(queries, keys, values, forward_out, out_grad, span_ids):
    me = lax.axis_index("ctx")
    my_x, my_z, my_y = me // (NZ * NY), (me // NY) % NZ, me % NY
    where = jnp.stack([my_x, my_z, my_y]).astype(jnp.int32)
    carried = ((SPAN + 16, 2 * WIDTH), BF16)
    sem = pltpu.SemaphoreType.DMA
    local = pltpu.VMEM((2 * SPAN, WIDTH), BF16)
    kept, sent = run(
        pack_kernel, [span_ids, where], [keys, values], [carried] * 2, [local, local, sem, sem],
        10, "pack", far=(0, 1),
    )
    given = shift(sent, dy=1)
    block, meta = run(
        join_kernel, [span_ids, where], [kept, given],
        [((BLOCK, 2 * WIDTH), BF16), ((5,), jnp.int32)], [], 10, "join", scalar_outs=(1,),
    )

    block, queries, out_grad, forward_out = lax.optimization_barrier(
        (block, queries, out_grad, forward_out)
    )
    q_other = shift(queries, dy=1)
    g_other = shift(out_grad, dy=1)
    qs, gs, qt, gt, delta = run(
        own_rows_kernel, [], [queries, out_grad, forward_out],
        [WIDE, WIDE, TALL, TALL, ((8, COLS // 2), F32)], [], 10**9, "own_rows",
    )
    below, above, across = shift(block, dz=1), shift(block, dz=-1), shift(block, dz=NZ // 2)
    below, above, across, qs, gs, qt, gt, delta = lax.optimization_barrier(
        (below, above, across, qs, gs, qt, gt, delta)
    )
    further = [
        shift(jnp.concatenate([across, below], axis=0), dz=1),
        shift(jnp.concatenate([across, above], axis=0), dz=-1),
    ]
    plane = jnp.concatenate([block, across, below, above] + further, axis=0)
    qs, qt = other_rows(q_other, qs, qt)
    gs, gt = other_rows(g_other, gs, gt)
    near, far, back = (shift(plane, dx=d) for d in range(1, NX))
    gathered = [plane, near, back, far]
    stats = None
    for i, part in enumerate(gathered):
        last = i == len(gathered) - 1
        stats = statistics(meta, [part], qt, stats, delta if last else None)
    other_stats = shift(stats, dy=1)
    pairs, *state = run(
        functools.partial(sort_kernel, len(gathered)), [], gathered,
        [((KEYS, 2 * WIDTH), BF16), SUMS, DQT], [], 10**9, "sort",
    )

    arrays = [pairs, qs, gs, qt, gt, stats, other_stats]
    *state, far = gradients(0, meta, arrays, state, BF16)
    far = shift(far, dx=ORDER[0])
    *state, up, down = gradients(1, meta, arrays, state, BF16)
    up, down = shift(up, dx=1), shift(down, dx=-1)
    far, *state = lax.optimization_barrier((far, *state))
    *state, own = gradients(2, meta, arrays, state, F32)
    dqt = state[1]
    over_x = [own, far, up, down]
    dq_own, dq_sent = run(
        d_queries_kernel, [], [dqt], [(OWN, F32), (OWN, BF16)], [], 10**8, "d_queries"
    )

    over_x = sum(part.astype(F32) for part in over_x).astype(BF16)
    over_x, dq_own, dq_sent = lax.optimization_barrier((over_x, dq_own, dq_sent))
    pair = 2 * SPAN
    over_z = over_x[:pair].astype(F32)
    for d in range(1, NZ):
        over_z += shift(over_x[d * pair : (d + 1) * pair], dz=d).astype(F32)
    dq_given = shift(dq_sent, dy=1)
    over_z, dq_given = lax.optimization_barrier((over_z, dq_given))
    d_queries = (dq_own + dq_given.astype(F32)).astype(BF16)
    first = my_y == 0
    upper, lower = over_z[:SPAN], over_z[SPAN:]
    given = shift(jnp.where(first, lower, upper), dy=1)
    final = jnp.where(
        first,
        jnp.concatenate([upper, given], axis=0),
        jnp.concatenate([given, lower], axis=0),
    )
    return (d_queries, final[:, :WIDTH] * FACTOR, final[:, WIDTH:])


def solution(mesh):
    rows = P(("dp", "ctx"), None)
    return jax.shard_map(
        per_device,
        mesh=mesh,
        in_specs=(rows, rows, rows, rows, rows, P(("dp", "ctx"))),
        out_specs=(rows, rows, rows),
        check_vma=False,
    )
```

```python
import functools
import math

import jax
import jax.numpy as jnp
from jax import lax
from jax.experimental import pallas as pl
from jax.experimental.pallas import tpu as pltpu
from jax.sharding import PartitionSpec as P

NX, NZ, NY = 4, 8, 2
DEVICES = NX * NZ * NY
SPAN = 64
SPANS = 2 * DEVICES
WIDTH = 128
HEADS = 12
ROWS = HEADS * SPAN
KINDS = 2 * NY
COLS = KINDS * ROWS
KEYS = SPANS // NY * SPAN
STATS_TILE = 8 * SPAN
TILE = 8 * SPAN
BLOCK = 2 * SPAN + 16
FACTOR = 1.0 / math.sqrt(WIDTH)
SCALE = FACTOR * math.log2(math.e)
NEG = -1e30
SAFE = 64.0
VMEM_LIMIT = 28 * 1024 * 1024

F32 = jnp.float32
BF16 = jnp.bfloat16


def place(x, z, y):
    return ((x % NX) * NZ + z % NZ) * NY + y % NY


def shift(block, dx=0, dz=0, dy=0):
    pairs = [
        (place(x, z, y), place(x + dx, z + dz, y + dy))
        for x in range(NX)
        for z in range(NZ)
        for y in range(NY)
    ]
    return lax.ppermute(block, "ctx", pairs)


def spans_of(meta):
    return meta[0], SPANS - 1 - meta[0], meta[1], SPANS - 1 - meta[1]


def pick(spans, kind):
    result = spans[0]
    for i in range(1, KINDS):
        result = jnp.where(kind == i, spans[i], result)
    return result


def columns(start, width=ROWS):
    return pl.ds(pl.multiple_of(start, WIDTH), width)


def numbers_rows(first, second):
    index = lax.broadcasted_iota(jnp.int32, (16, 2 * WIDTH), 0)
    return jnp.where(index < 8, first, second).astype(F32).astype(BF16)


def pack_kernel(ids, where, keys_any, values_any, kept, sent, keys, values, sem, sem_v):
    copies = [
        pltpu.make_async_copy(keys_any, keys, sem),
        pltpu.make_async_copy(values_any, values, sem_v),
    ]
    for copy in copies:
        copy.start()
    for copy in copies:
        copy.wait()
    keep = jnp.where((ids[0] & 1) == where[2], 0, 1)
    for target, slot in ((kept, keep), (sent, 1 - keep)):
        rows = pl.ds(pl.multiple_of(slot * SPAN, SPAN), SPAN)
        target[:SPAN, :WIDTH] = keys[rows, :]
        target[:SPAN, WIDTH:] = values[rows, :]
        number = jnp.where(slot == 0, ids[0], ids[1])
        target[SPAN:, :] = numbers_rows(number, ids[0])


def join_kernel(ids, where, kept, given, block, meta):
    block[:SPAN, :] = kept[:SPAN, :]
    block[SPAN : 2 * SPAN, :] = given[:SPAN, :]
    mine, other = kept[SPAN:, :].astype(F32), given[SPAN:, :].astype(F32)
    block[2 * SPAN :, :] = jnp.concatenate([mine[:8], other[:8]], axis=0).astype(BF16)
    meta[0] = ids[0]
    meta[1] = other[8, 0].astype(jnp.int32)
    for i in range(3):
        meta[2 + i] = where[i]


def place_heads(own, refs, sources):
    for slot in range(2):
        rows = slice(slot * SPAN, (slot + 1) * SPAN)
        for b in range(HEADS // 2):
            lanes = [slice(h * WIDTH, (h + 1) * WIDTH) for h in (2 * b, 2 * b + 1)]
            start = ((0 if own else 2) + slot) * ROWS + b * WIDTH
            target = slice(start, start + WIDTH)
            blocks = []
            for source in sources:
                blocks.append(jnp.concatenate([source[rows, i] for i in lanes], axis=0))
            for (tall, wide), block in zip(refs, blocks):
                wide[target, :] = block
                tall[:, target] = block.T
            if own:
                yield target, blocks


def own_rows_kernel(q_own, g_own, o_own, qs, gs, qt, gt, delta):
    for target, (_, g, o) in place_heads(True, ((qt, qs), (gt, gs)), (q_own, g_own, o_own)):
        total = jnp.sum((g.astype(F32) * o.astype(F32)).T, axis=0, keepdims=True)
        delta[:, target] = jnp.broadcast_to(total, (8, WIDTH))


def other_rows_kernel(rows, _wide, _tall, wide, tall):
    for _ in place_heads(False, ((tall, wide),), (rows,)):
        pass


def plane_kernel(*refs):
    pieces, plane = refs[:-1], refs[-1]
    index = lax.broadcasted_iota(jnp.int32, (16, 2 * WIDTH), 0)
    numbers = jnp.zeros((16, 2 * WIDTH), F32)
    count = 0
    for piece in pieces:
        for b in range(piece.shape[0] // BLOCK):
            start = b * BLOCK
            plane[count * SPAN : (count + 2) * SPAN, :] = piece[start : start + 2 * SPAN, :]
            tail = piece[start + 2 * SPAN : start + BLOCK, :].astype(F32)
            numbers = jnp.where(index == count, tail[0:1], numbers)
            numbers = jnp.where(index == count + 1, tail[8:9], numbers)
            count += 2
    plane[count * SPAN :, :] = numbers.astype(BF16)


def read_numbers(parts):
    found = []
    for part in parts:
        tail = part[2 * NZ * SPAN :, :WIDTH].astype(F32)
        for i in range(2 * NZ):
            found.append((tail[i, 0].astype(jnp.int32), part, i * SPAN))
    return found


def sort_kernel(n_parts, *refs):
    parts, (pairs, sums, dqt) = refs[:n_parts], refs[n_parts:]
    sums[...] = jnp.zeros(sums.shape, F32)
    dqt[...] = jnp.zeros(dqt.shape, F32)
    for number, part, row in read_numbers(parts):
        target = pl.multiple_of(number // NY * SPAN, SPAN)
        pairs[pl.ds(target, SPAN), :] = part[row : row + SPAN, :]


def hidden(offsets, shape):
    index = lax.broadcasted_iota(jnp.int32, shape, 0)
    offset = offsets[0]
    for i in range(1, len(offsets)):
        offset = jnp.where(index >= i * SPAN, offsets[i], offset)
    row = lax.broadcasted_iota(jnp.int32, shape, 1) & (SPAN - 1)
    return offset * SPAN + (index & (SPAN - 1)) > row


def statistics_kernel(n_parts, first, last, meta, *refs):
    parts, refs = refs[:n_parts], list(refs[n_parts:])
    qt = refs.pop(0)
    before_ref = None if first else refs.pop(0)
    delta = refs.pop(0) if last else None
    out, row_max, row_sum, base, top, extra, keys, ordered = refs
    spans = spans_of(meta)
    found = read_numbers(parts)
    for number, part, row in found:
        rank = sum((other < number).astype(jnp.int32) for other, _, _ in found)
        ordered[rank] = number
        target = pl.multiple_of(rank * SPAN, SPAN)
        keys[pl.ds(target, SPAN), :] = part[row : row + SPAN, :WIDTH]
    if first:
        row_max[...] = jnp.full((8, COLS), NEG, F32)
        row_sum[...] = jnp.zeros((8, COLS), F32)
    else:
        row_max[...] = before_ref[:8, :]
        row_sum[...] = before_ref[8:, :]
    group = STATS_TILE // SPAN

    def visit_all(visit, width, always_masked):
        def step(i, carry):
            kind = i // (ROWS // width)
            span = pick(spans, kind)
            cols = columns(i * width, width)

            def scores(tile, masked):
                k = keys[pl.ds(pl.multiple_of(tile * STATS_TILE, STATS_TILE), STATS_TILE), :]
                s = jnp.dot(k, qt[:, cols], preferred_element_type=F32) * SCALE
                if masked:
                    offsets = [ordered[tile * group + i] - span for i in range(group)]
                    s = jnp.where(hidden(offsets, s.shape), 2 * NEG, s)
                visit(s.reshape(STATS_TILE // 8, 8, width), cols)

            full = sum((number < span).astype(jnp.int32) for number, _, _ in found) // group
            seen = sum((number <= span).astype(jnp.int32) for number, _, _ in found)
            if always_masked:
                tiles = (seen + group - 1) // group
                lax.fori_loop(0, tiles, lambda t, c: scores(t, True), None)
                return carry
            lax.fori_loop(0, full, lambda t, c: scores(t, False), None)

            @pl.when(seen > full * group)
            def _():
                scores(full, True)

            return carry

        lax.fori_loop(0, COLS // width, step, 0)

    def against_base(s, cols):
        top[:, cols] = jnp.maximum(top[:, cols], jnp.max(s, axis=0))
        extra[:, cols] += jnp.sum(jnp.exp2(s - base[:, cols][None]), axis=0)

    def against_maximum(s, cols):
        before = row_max[:, cols]
        after = jnp.maximum(before, jnp.max(s, axis=0))
        fresh = jnp.sum(jnp.exp2(s - after[None]), axis=0)
        row_sum[:, cols] = row_sum[:, cols] * jnp.exp2(before - after) + fresh
        row_max[:, cols] = after

    unset = row_max[...] <= NEG
    base[...] = jnp.where(unset, 0.0, row_max[...])
    top[...] = jnp.full((8, COLS), 2 * NEG, F32)
    extra[...] = jnp.zeros((8, COLS), F32)
    visit_all(against_base, ROWS, False)
    unset = row_max[...] <= NEG
    seen = top[...] > NEG
    gap = top[...] - base[...]
    far = seen & ((gap > SAFE) | (unset & (gap < -SAFE)))
    any_far = jnp.max(jnp.where(far, 1.0, 0.0)) > 0.0

    @pl.when(jnp.logical_not(any_far))
    def _():
        empty = unset & jnp.logical_not(seen)
        after = jnp.maximum(base[...], top[...])
        total = (row_sum[...] + extra[...]) * jnp.exp2(base[...] - after)
        row_sum[...] = jnp.where(empty, 0.0, total)
        row_max[...] = jnp.where(empty, NEG, after)

    @pl.when(any_far)
    def _():
        visit_all(against_maximum, WIDTH, True)

    if not last:
        out[:8, :] = row_max[...]
        out[8:, :] = row_sum[...]
    else:
        most = jnp.max(row_max[...], axis=0, keepdims=True)
        total = jnp.sum(row_sum[...] * jnp.exp2(row_max[...] - most), axis=0, keepdims=True)
        out[0:1, :] = most
        out[1:2, :] = total
        out[2:3, : 2 * ROWS] = delta[0:1, :]
        out[2:3, 2 * ROWS :] = jnp.zeros((1, 2 * ROWS), F32)
        out[3:8, :] = jnp.zeros((5, COLS), F32)


ORDER = (2, 1, NX - 1, 0)
TILES = KEYS // NX // TILE
STAGES = ((0,), (1, 2), (3,))


Z_ORDER = (0, 4, 1, 7, 5, 2, 3, 6)


def gradients_kernel(stage, meta, pairs, qs, gs, qt, gt, mine_ref, other_ref, _sums, _dqt, *refs):
    sums, dqt = refs[:2]
    outs, (level, delta) = refs[2:-2], refs[-2:]
    spans = spans_of(meta)
    my_x, my_z, parity = meta[2], meta[3], meta[4]
    half = 2 * ROWS
    for mine, other in ((slice(0, half), slice(half, COLS)), (slice(half, COLS), slice(0, half))):
        top = jnp.maximum(mine_ref[0:1, mine], other_ref[0:1, other])
        total = mine_ref[1:2, mine] * jnp.exp2(mine_ref[0:1, mine] - top)
        total += other_ref[1:2, other] * jnp.exp2(other_ref[0:1, other] - top)
        level[:, mine] = top + jnp.log2(total)
        delta[:, mine] = mine_ref[2:3, mine] + other_ref[2:3, other]
    group = TILE // SPAN
    lasts = [jnp.maximum(span - parity, 0) // NY // group for span in spans]
    firsts = [(my_x + off) % NX * TILES for off in ORDER]
    counts = [
        sum(jnp.clip(last - first + 1, 0, TILES) for last in lasts) for first in firsts
    ]
    ready = [sum(counts[: entries[-1] + 1]) for entries in STAGES]
    everything = ready[-1]
    ends = [
        jnp.maximum(needed, (everything * (i + 1) + len(STAGES) - 1) // len(STAGES))
        for i, needed in enumerate(ready)
    ]
    begin = 0 if stage == 0 else ends[stage - 1]
    end = ends[stage]

    def visit(kind, tile, masked):
        span = pick(spans, kind)
        cols = columns(kind * ROWS)
        rows = pl.ds(pl.multiple_of(tile * TILE, TILE), TILE)
        k = pairs[rows, :WIDTH]
        v = pairs[rows, WIDTH:]
        s = jnp.dot(k, qt[:, cols], preferred_element_type=F32) * SCALE
        p = jnp.exp2(s - level[:, cols])
        if masked:
            offsets = [(tile * group + j) * NY + parity - span for j in range(group)]
            p = jnp.where(hidden(offsets, p.shape), 0.0, p)
        dp = jnp.dot(v, gt[:, cols], preferred_element_type=F32)
        ds = (p * (dp - delta[:, cols])).astype(BF16)
        d_value = jnp.dot(p.astype(BF16), gs[cols, :], preferred_element_type=F32)
        d_key = jnp.dot(ds, qs[cols, :], preferred_element_type=F32)
        dqt[:, cols] += jnp.dot(k.T, ds, preferred_element_type=F32)
        sums[rows, :WIDTH] += d_key
        sums[rows, WIDTH:] += d_value

    def step(i, done):
        entry, kind = i // KINDS, i % KINDS
        first, last = pick(firsts, entry), pick(lasts, kind)
        count = jnp.clip(last - first + 1, 0, TILES)

        def part_step(part, carry):
            tile = first + part

            @pl.when(tile < last)
            def _():
                visit(kind, tile, False)

            @pl.when(tile == last)
            def _():
                visit(kind, tile, True)

            return carry

        low, high = jnp.clip(begin - done, 0, count), jnp.clip(end - done, 0, count)
        lax.fori_loop(low, high, part_step, 0)
        return done + count

    lax.fori_loop(0, len(ORDER) * KINDS, step, jnp.int32(0))
    pair = 2 * SPAN
    for entry, out in zip(STAGES[stage], outs):
        for i, z_off in enumerate(Z_ORDER):
            start = firsts[entry] * TILE + (my_z + z_off) % NZ * pair
            source = pl.ds(pl.multiple_of(start, pair), pair)
            out[i * pair : (i + 1) * pair, :] = sums[source, :].astype(out.dtype)


def d_queries_kernel(dqt, dq_own, dq_other):
    for device, out in enumerate((dq_own, dq_other)):
        for slot in range(2):
            for b in range(ROWS // WIDTH):
                start = (2 * device + slot) * ROWS + b * WIDTH
                block = dqt[:, start : start + WIDTH].T * FACTOR
                for half in range(2):
                    h = 2 * b + half
                    out[slot * SPAN : (slot + 1) * SPAN, h * WIDTH : (h + 1) * WIDTH] = block[
                        half * SPAN : (half + 1) * SPAN
                    ].astype(out.dtype)


def run(kernel, scalars, arrays, outs, scratch, flops, name, far=(), aliases=None, scalar_outs=()):
    spaces = [pltpu.SMEM] * len(scalars)
    spaces += [pltpu.HBM if i in far else pltpu.VMEM for i in range(len(arrays))]
    return pl.pallas_call(
        kernel,
        out_shape=[jax.ShapeDtypeStruct(s, d) for s, d in outs],
        in_specs=[pl.BlockSpec(memory_space=space) for space in spaces],
        out_specs=[
            pl.BlockSpec(memory_space=pltpu.SMEM if i in scalar_outs else pltpu.VMEM)
            for i in range(len(outs))
        ],
        scratch_shapes=scratch,
        input_output_aliases=aliases or {},
        compiler_params=pltpu.CompilerParams(vmem_limit_bytes=VMEM_LIMIT),
        cost_estimate=pl.CostEstimate(flops=flops, bytes_accessed=10**5, transcendentals=0),
        name=name,
    )(*scalars, *arrays)


WIDE = ((COLS, WIDTH), BF16)
TALL = ((WIDTH, COLS), BF16)
FLAT = ((8, COLS), F32)
OWN = (2 * SPAN, HEADS * WIDTH)
SUMS = ((KEYS, 2 * WIDTH), F32)
DQT = ((WIDTH, COLS), F32)


def statistics(meta, parts, qt, before, delta):
    first, last = before is None, delta is not None
    count = 2 * NZ * len(parts)
    arrays = list(parts) + [qt] + [a for a in (before, delta) if a is not None]
    return run(
        functools.partial(statistics_kernel, len(parts), first, last),
        [meta],
        arrays,
        [FLAT if last else ((16, COLS), F32)],
        [pltpu.VMEM((8, COLS), F32)] * 5
        + [pltpu.VMEM((count * SPAN, WIDTH), BF16), pltpu.SMEM((count,), jnp.int32)],
        2 * 10**9,
        "row_statistics",
    )[0]


def other_rows(rows, wide, tall):
    return run(
        other_rows_kernel, [], [rows, wide, tall], [WIDE, TALL], [], 10**9, "other_rows",
        aliases={1: 0, 2: 1},
    )


def gradients(stage, meta, arrays, state, dtype):
    share = ((KEYS // NX, 2 * WIDTH), dtype)
    count = 1 + len(arrays)
    return run(
        functools.partial(gradients_kernel, stage),
        [meta],
        arrays + list(state),
        [SUMS, DQT] + [share] * len(STAGES[stage]),
        [pltpu.VMEM((1, COLS), F32)] * 2,
        8 * 10**9,
        "gradients",
        aliases={count: 0, count + 1: 1},
    )


def per_device(queries, keys, values, forward_out, out_grad, span_ids):
    me = lax.axis_index("ctx")
    my_x, my_z, my_y = me // (NZ * NY), (me // NY) % NZ, me % NY
    where = jnp.stack([my_x, my_z, my_y]).astype(jnp.int32)
    carried = ((SPAN + 16, 2 * WIDTH), BF16)
    sem = pltpu.SemaphoreType.DMA
    local = pltpu.VMEM((2 * SPAN, WIDTH), BF16)
    kept, sent = run(
        pack_kernel, [span_ids, where], [keys, values], [carried] * 2, [local, local, sem, sem],
        10, "pack", far=(0, 1),
    )
    given = shift(sent, dy=1)
    block, meta = run(
        join_kernel, [span_ids, where], [kept, given],
        [((BLOCK, 2 * WIDTH), BF16), ((5,), jnp.int32)], [], 10, "join", scalar_outs=(1,),
    )

    block, queries, out_grad, forward_out = lax.optimization_barrier(
        (block, queries, out_grad, forward_out)
    )
    q_other = shift(queries, dy=1)
    g_other = shift(out_grad, dy=1)
    qs, gs, qt, gt, delta = run(
        own_rows_kernel, [], [queries, out_grad, forward_out],
        [WIDE, WIDE, TALL, TALL, ((8, COLS // 2), F32)], [], 10**9, "own_rows",
    )
    below, above, across = shift(block, dz=1), shift(block, dz=-1), shift(block, dz=NZ // 2)
    below, above, across, qs, gs, qt, gt, delta = lax.optimization_barrier(
        (below, above, across, qs, gs, qt, gt, delta)
    )
    further = [
        shift(jnp.concatenate([across, below], axis=0), dz=1),
        shift(jnp.concatenate([across, above], axis=0), dz=-1),
    ]
    (plane,) = run(
        plane_kernel, [], [block, across, below, above] + further,
        [((2 * NZ * SPAN + 16, 2 * WIDTH), BF16)], [], 10, "plane",
    )
    qs, qt = other_rows(q_other, qs, qt)
    gs, gt = other_rows(g_other, gs, gt)
    near, far, back = (shift(plane, dx=d) for d in range(1, NX))
    gathered = [plane, near, back, far]
    stats = None
    for i, part in enumerate(gathered):
        last = i == len(gathered) - 1
        stats = statistics(meta, [part], qt, stats, delta if last else None)
    other_stats = shift(stats, dy=1)
    pairs, *state = run(
        functools.partial(sort_kernel, len(gathered)), [], gathered,
        [((KEYS, 2 * WIDTH), BF16), SUMS, DQT], [], 10**9, "sort",
    )

    arrays = [pairs, qs, gs, qt, gt, stats, other_stats]
    *state, far = gradients(0, meta, arrays, state, BF16)
    far = shift(far, dx=ORDER[0])
    *state, up, down = gradients(1, meta, arrays, state, BF16)
    up, down = shift(up, dx=1), shift(down, dx=-1)
    far, *state = lax.optimization_barrier((far, *state))
    *state, own = gradients(2, meta, arrays, state, F32)
    dqt = state[1]
    over_x = [own, far, up, down]
    dq_own, dq_sent = run(
        d_queries_kernel, [], [dqt], [(OWN, F32), (OWN, BF16)], [], 10**8, "d_queries"
    )

    over_x = sum(part.astype(F32) for part in over_x)
    over_x, dq_own, dq_sent = lax.optimization_barrier((over_x, dq_own, dq_sent))
    pair = 2 * SPAN
    mine, across, above, below, up, down = (
        over_x[a * pair : b * pair] for a, b in ((0, 1), (1, 2), (2, 3), (3, 4), (4, 6), (6, 8))
    )
    from_below = shift(up.astype(BF16), dz=1).astype(F32)
    from_above = shift(down.astype(BF16), dz=-1).astype(F32)
    across = across + from_below[:pair] + from_above[:pair]
    above = above + from_below[pair:]
    below = below + from_above[pair:]
    over_z = mine
    for part, d in ((across, NZ // 2), (above, 1), (below, -1)):
        over_z = over_z + shift(part.astype(BF16), dz=d).astype(F32)
    dq_given = shift(dq_sent, dy=1)
    over_z, dq_given = lax.optimization_barrier((over_z, dq_given))
    d_queries = (dq_own + dq_given.astype(F32)).astype(BF16)
    first = my_y == 0
    upper, lower = over_z[:SPAN], over_z[SPAN:]
    given = shift(jnp.where(first, lower, upper), dy=1)
    final = jnp.where(
        first,
        jnp.concatenate([upper, given], axis=0),
        jnp.concatenate([given, lower], axis=0),
    )
    return (d_queries, final[:, :WIDTH] * FACTOR, final[:, WIDTH:])


def solution(mesh):
    rows = P(("dp", "ctx"), None)
    return jax.shard_map(
        per_device,
        mesh=mesh,
        in_specs=(rows, rows, rows, rows, rows, P(("dp", "ctx"))),
        out_specs=(rows, rows, rows),
        check_vma=False,
    )
```

```python
import functools
import math

import jax
import jax.numpy as jnp
from jax import lax
from jax.experimental import pallas as pl
from jax.experimental.pallas import tpu as pltpu
from jax.sharding import PartitionSpec as P

NX, NZ, NY = 4, 8, 2
DEVICES = NX * NZ * NY
SPAN = 64
SPANS = 2 * DEVICES
WIDTH = 128
HEADS = 12
ROWS = HEADS * SPAN
KINDS = 2 * NY
COLS = KINDS * ROWS
KEYS = SPANS // NY * SPAN
STATS_TILE = 8 * SPAN
TILE = 8 * SPAN
BLOCK = 2 * SPAN + 16
FACTOR = 1.0 / math.sqrt(WIDTH)
SCALE = FACTOR * math.log2(math.e)
NEG = -1e30
SAFE = 64.0
VMEM_LIMIT = 28 * 1024 * 1024

F32 = jnp.float32
BF16 = jnp.bfloat16


def place(x, z, y):
    return ((x % NX) * NZ + z % NZ) * NY + y % NY


def shift(block, dx=0, dz=0, dy=0):
    pairs = [
        (place(x, z, y), place(x + dx, z + dz, y + dy))
        for x in range(NX)
        for z in range(NZ)
        for y in range(NY)
    ]
    return lax.ppermute(block, "ctx", pairs)


def spans_of(meta):
    return meta[0], SPANS - 1 - meta[0], meta[1], SPANS - 1 - meta[1]


def pick(spans, kind):
    result = spans[0]
    for i in range(1, KINDS):
        result = jnp.where(kind == i, spans[i], result)
    return result


def columns(start, width=ROWS):
    return pl.ds(pl.multiple_of(start, WIDTH), width)


def numbers_rows(first, second):
    index = lax.broadcasted_iota(jnp.int32, (16, 2 * WIDTH), 0)
    return jnp.where(index < 8, first, second).astype(F32).astype(BF16)


def pack_kernel(ids, where, keys_any, values_any, kept, sent, keys, values, sem, sem_v):
    copies = [
        pltpu.make_async_copy(keys_any, keys, sem),
        pltpu.make_async_copy(values_any, values, sem_v),
    ]
    for copy in copies:
        copy.start()
    for copy in copies:
        copy.wait()
    keep = jnp.where((ids[0] & 1) == where[2], 0, 1)
    for target, slot in ((kept, keep), (sent, 1 - keep)):
        rows = pl.ds(pl.multiple_of(slot * SPAN, SPAN), SPAN)
        target[:SPAN, :WIDTH] = keys[rows, :]
        target[:SPAN, WIDTH:] = values[rows, :]
        number = jnp.where(slot == 0, ids[0], ids[1])
        target[SPAN:, :] = numbers_rows(number, ids[0])


def join_kernel(ids, where, kept, given, block, meta):
    block[:SPAN, :] = kept[:SPAN, :]
    block[SPAN : 2 * SPAN, :] = given[:SPAN, :]
    mine, other = kept[SPAN:, :].astype(F32), given[SPAN:, :].astype(F32)
    block[2 * SPAN :, :] = jnp.concatenate([mine[:8], other[:8]], axis=0).astype(BF16)
    meta[0] = ids[0]
    meta[1] = other[8, 0].astype(jnp.int32)
    for i in range(3):
        meta[2 + i] = where[i]


def place_heads(own, refs, sources):
    for slot in range(2):
        rows = slice(slot * SPAN, (slot + 1) * SPAN)
        for b in range(HEADS // 2):
            lanes = [slice(h * WIDTH, (h + 1) * WIDTH) for h in (2 * b, 2 * b + 1)]
            start = ((0 if own else 2) + slot) * ROWS + b * WIDTH
            target = slice(start, start + WIDTH)
            blocks = []
            for source in sources:
                blocks.append(jnp.concatenate([source[rows, i] for i in lanes], axis=0))
            for (tall, wide), block in zip(refs, blocks):
                wide[target, :] = block
                tall[:, target] = block.T
            if own:
                yield target, blocks


def own_rows_kernel(q_own, g_own, o_own, qs, gs, qt, gt, delta):
    for target, (_, g, o) in place_heads(True, ((qt, qs), (gt, gs)), (q_own, g_own, o_own)):
        total = jnp.sum((g.astype(F32) * o.astype(F32)).T, axis=0, keepdims=True)
        delta[:, target] = jnp.broadcast_to(total, (8, WIDTH))


def other_rows_kernel(rows, _wide, _tall, wide, tall):
    for _ in place_heads(False, ((tall, wide),), (rows,)):
        pass


def plane_kernel(*refs):
    pieces, plane = refs[:-1], refs[-1]
    index = lax.broadcasted_iota(jnp.int32, (16, 2 * WIDTH), 0)
    numbers = jnp.zeros((16, 2 * WIDTH), F32)
    count = 0
    for piece in pieces:
        for b in range(piece.shape[0] // BLOCK):
            start = b * BLOCK
            plane[count * SPAN : (count + 2) * SPAN, :] = piece[start : start + 2 * SPAN, :]
            tail = piece[start + 2 * SPAN : start + BLOCK, :].astype(F32)
            numbers = jnp.where(index == count, tail[0:1], numbers)
            numbers = jnp.where(index == count + 1, tail[8:9], numbers)
            count += 2
    plane[count * SPAN :, :] = numbers.astype(BF16)


def read_numbers(parts):
    found = []
    for part in parts:
        tail = part[2 * NZ * SPAN :, :WIDTH].astype(F32)
        for i in range(2 * NZ):
            found.append((tail[i, 0].astype(jnp.int32), part, i * SPAN))
    return found


def sort_kernel(n_parts, *refs):
    parts, (pairs, sums, dqt) = refs[:n_parts], refs[n_parts:]
    sums[...] = jnp.zeros(sums.shape, F32)
    dqt[...] = jnp.zeros(dqt.shape, F32)
    for number, part, row in read_numbers(parts):
        target = pl.multiple_of(number // NY * SPAN, SPAN)
        pairs[pl.ds(target, SPAN), :] = part[row : row + SPAN, :]


def hide(scores, offsets):
    shape = (scores.shape[0], WIDTH)
    index = lax.broadcasted_iota(jnp.int32, shape, 0)
    offset = jnp.full(shape, offsets[0], jnp.int32)
    for i in range(1, len(offsets)):
        offset = jnp.where(index >= i * SPAN, offsets[i], offset)
    row = lax.broadcasted_iota(jnp.int32, shape, 1) & (SPAN - 1)
    lowered = jnp.where(offset * SPAN + (index & (SPAN - 1)) > row, 2 * NEG, 0.0)
    return scores + jnp.concatenate([lowered] * (scores.shape[1] // WIDTH), axis=1)


def statistics_kernel(n_parts, first, last, meta, *refs):
    parts, refs = refs[:n_parts], list(refs[n_parts:])
    qt = refs.pop(0)
    before_ref = None if first else refs.pop(0)
    delta = refs.pop(0) if last else None
    out, row_max, row_sum, base, top, extra, keys, ordered = refs
    spans = spans_of(meta)
    found = read_numbers(parts)
    for number, part, row in found:
        rank = sum((other < number).astype(jnp.int32) for other, _, _ in found)
        ordered[rank] = number
        target = pl.multiple_of(rank * SPAN, SPAN)
        keys[pl.ds(target, SPAN), :] = part[row : row + SPAN, :WIDTH]
    if first:
        row_max[...] = jnp.full((8, COLS), NEG, F32)
        row_sum[...] = jnp.zeros((8, COLS), F32)
    else:
        row_max[...] = before_ref[:8, :]
        row_sum[...] = before_ref[8:, :]
    group = STATS_TILE // SPAN

    def visit_all(visit, width, always_masked):
        def step(i, carry):
            kind = i // (ROWS // width)
            span = pick(spans, kind)
            cols = columns(i * width, width)

            def scores(tile, masked):
                k = keys[pl.ds(pl.multiple_of(tile * STATS_TILE, STATS_TILE), STATS_TILE), :]
                s = jnp.dot(k, qt[:, cols], preferred_element_type=F32) * SCALE
                if masked:
                    offsets = [ordered[tile * group + i] - span for i in range(group)]
                    s = hide(s, offsets)
                visit(s.reshape(STATS_TILE // 8, 8, width), cols)

            full = sum((number < span).astype(jnp.int32) for number, _, _ in found) // group
            seen = sum((number <= span).astype(jnp.int32) for number, _, _ in found)
            if always_masked:
                tiles = (seen + group - 1) // group
                lax.fori_loop(0, tiles, lambda t, c: scores(t, True), None)
                return carry
            lax.fori_loop(0, full, lambda t, c: scores(t, False), None)

            @pl.when(seen > full * group)
            def _():
                scores(full, True)

            return carry

        lax.fori_loop(0, COLS // width, step, 0)

    def against_base(s, cols):
        top[:, cols] = jnp.maximum(top[:, cols], jnp.max(s, axis=0))
        extra[:, cols] += jnp.sum(jnp.exp2(s - base[:, cols][None]), axis=0)

    def against_maximum(s, cols):
        before = row_max[:, cols]
        after = jnp.maximum(before, jnp.max(s, axis=0))
        fresh = jnp.sum(jnp.exp2(s - after[None]), axis=0)
        row_sum[:, cols] = row_sum[:, cols] * jnp.exp2(before - after) + fresh
        row_max[:, cols] = after

    unset = row_max[...] <= NEG
    base[...] = jnp.where(unset, 0.0, row_max[...])
    top[...] = jnp.full((8, COLS), 2 * NEG, F32)
    extra[...] = jnp.zeros((8, COLS), F32)
    visit_all(against_base, ROWS, False)
    unset = row_max[...] <= NEG
    seen = top[...] > NEG
    gap = top[...] - base[...]
    far = seen & ((gap > SAFE) | (unset & (gap < -SAFE)))
    any_far = jnp.max(jnp.where(far, 1.0, 0.0)) > 0.0

    @pl.when(jnp.logical_not(any_far))
    def _():
        empty = unset & jnp.logical_not(seen)
        after = jnp.maximum(base[...], top[...])
        total = (row_sum[...] + extra[...]) * jnp.exp2(base[...] - after)
        row_sum[...] = jnp.where(empty, 0.0, total)
        row_max[...] = jnp.where(empty, NEG, after)

    @pl.when(any_far)
    def _():
        visit_all(against_maximum, WIDTH, True)

    if not last:
        out[:8, :] = row_max[...]
        out[8:, :] = row_sum[...]
    else:
        most = jnp.max(row_max[...], axis=0, keepdims=True)
        total = jnp.sum(row_sum[...] * jnp.exp2(row_max[...] - most), axis=0, keepdims=True)
        out[0:1, :] = most
        out[1:2, :] = total
        out[2:3, : 2 * ROWS] = delta[0:1, :]
        out[2:3, 2 * ROWS :] = jnp.zeros((1, 2 * ROWS), F32)
        out[3:8, :] = jnp.zeros((5, COLS), F32)


ORDER = (2, 1, NX - 1, 0)
TILES = KEYS // NX // TILE
STAGES = ((0,), (1, 2), (3,))


Z_ORDER = (0, 4, 1, 7, 5, 2, 3, 6)


def gradients_kernel(stage, meta, pairs, qs, gs, qt, gt, mine_ref, other_ref, _sums, _dqt, *refs):
    sums, dqt = refs[:2]
    outs, (level, delta) = refs[2:-2], refs[-2:]
    spans = spans_of(meta)
    my_x, my_z, parity = meta[2], meta[3], meta[4]
    half = 2 * ROWS
    for mine, other in ((slice(0, half), slice(half, COLS)), (slice(half, COLS), slice(0, half))):
        top = jnp.maximum(mine_ref[0:1, mine], other_ref[0:1, other])
        total = mine_ref[1:2, mine] * jnp.exp2(mine_ref[0:1, mine] - top)
        total += other_ref[1:2, other] * jnp.exp2(other_ref[0:1, other] - top)
        level[:, mine] = top + jnp.log2(total)
        delta[:, mine] = mine_ref[2:3, mine] + other_ref[2:3, other]
    group = TILE // SPAN
    lasts = [jnp.maximum(span - parity, 0) // NY // group for span in spans]
    firsts = [(my_x + off) % NX * TILES for off in ORDER]
    counts = [
        sum(jnp.clip(last - first + 1, 0, TILES) for last in lasts) for first in firsts
    ]
    ready = [sum(counts[: entries[-1] + 1]) for entries in STAGES]
    everything = ready[-1]
    ends = [
        jnp.maximum(needed, (everything * (i + 1) + len(STAGES) - 1) // len(STAGES))
        for i, needed in enumerate(ready)
    ]
    begin = 0 if stage == 0 else ends[stage - 1]
    end = ends[stage]

    def visit(kind, tile, masked):
        span = pick(spans, kind)
        cols = columns(kind * ROWS)
        rows = pl.ds(pl.multiple_of(tile * TILE, TILE), TILE)
        k = pairs[rows, :WIDTH]
        v = pairs[rows, WIDTH:]
        s = jnp.dot(k, qt[:, cols], preferred_element_type=F32) * SCALE
        if masked:
            s = hide(s, [(tile * group + j) * NY + parity - span for j in range(group)])
        p = jnp.exp2(s - level[:, cols])
        dp = jnp.dot(v, gt[:, cols], preferred_element_type=F32)
        ds = (p * (dp - delta[:, cols])).astype(BF16)
        d_value = jnp.dot(p.astype(BF16), gs[cols, :], preferred_element_type=F32)
        d_key = jnp.dot(ds, qs[cols, :], preferred_element_type=F32)
        dqt[:, cols] += jnp.dot(k.T, ds, preferred_element_type=F32)
        sums[rows, :WIDTH] += d_key
        sums[rows, WIDTH:] += d_value

    def step(i, done):
        entry, kind = i // KINDS, i % KINDS
        first, last = pick(firsts, entry), pick(lasts, kind)
        count = jnp.clip(last - first + 1, 0, TILES)

        def part_step(part, carry):
            tile = first + part

            @pl.when(tile < last)
            def _():
                visit(kind, tile, False)

            @pl.when(tile == last)
            def _():
                visit(kind, tile, True)

            return carry

        low, high = jnp.clip(begin - done, 0, count), jnp.clip(end - done, 0, count)
        lax.fori_loop(low, high, part_step, 0)
        return done + count

    lax.fori_loop(0, len(ORDER) * KINDS, step, jnp.int32(0))
    pair = 2 * SPAN
    for entry, out in zip(STAGES[stage], outs):
        for i, z_off in enumerate(Z_ORDER):
            start = firsts[entry] * TILE + (my_z + z_off) % NZ * pair
            source = pl.ds(pl.multiple_of(start, pair), pair)
            out[i * pair : (i + 1) * pair, :] = sums[source, :].astype(out.dtype)


def d_queries_kernel(dqt, dq_own, dq_other):
    for device, out in enumerate((dq_own, dq_other)):
        for slot in range(2):
            for b in range(ROWS // WIDTH):
                start = (2 * device + slot) * ROWS + b * WIDTH
                block = dqt[:, start : start + WIDTH].T * FACTOR
                for half in range(2):
                    h = 2 * b + half
                    out[slot * SPAN : (slot + 1) * SPAN, h * WIDTH : (h + 1) * WIDTH] = block[
                        half * SPAN : (half + 1) * SPAN
                    ].astype(out.dtype)


def run(kernel, scalars, arrays, outs, scratch, flops, name, far=(), aliases=None, scalar_outs=()):
    spaces = [pltpu.SMEM] * len(scalars)
    spaces += [pltpu.HBM if i in far else pltpu.VMEM for i in range(len(arrays))]
    return pl.pallas_call(
        kernel,
        out_shape=[jax.ShapeDtypeStruct(s, d) for s, d in outs],
        in_specs=[pl.BlockSpec(memory_space=space) for space in spaces],
        out_specs=[
            pl.BlockSpec(memory_space=pltpu.SMEM if i in scalar_outs else pltpu.VMEM)
            for i in range(len(outs))
        ],
        scratch_shapes=scratch,
        input_output_aliases=aliases or {},
        compiler_params=pltpu.CompilerParams(vmem_limit_bytes=VMEM_LIMIT),
        cost_estimate=pl.CostEstimate(flops=flops, bytes_accessed=10**5, transcendentals=0),
        name=name,
    )(*scalars, *arrays)


WIDE = ((COLS, WIDTH), BF16)
TALL = ((WIDTH, COLS), BF16)
FLAT = ((8, COLS), F32)
OWN = (2 * SPAN, HEADS * WIDTH)
SUMS = ((KEYS, 2 * WIDTH), F32)
DQT = ((WIDTH, COLS), F32)


def statistics(meta, parts, qt, before, delta):
    first, last = before is None, delta is not None
    count = 2 * NZ * len(parts)
    arrays = list(parts) + [qt] + [a for a in (before, delta) if a is not None]
    return run(
        functools.partial(statistics_kernel, len(parts), first, last),
        [meta],
        arrays,
        [FLAT if last else ((16, COLS), F32)],
        [pltpu.VMEM((8, COLS), F32)] * 5
        + [pltpu.VMEM((count * SPAN, WIDTH), BF16), pltpu.SMEM((count,), jnp.int32)],
        2 * 10**9,
        "row_statistics",
    )[0]


def other_rows(rows, wide, tall):
    return run(
        other_rows_kernel, [], [rows, wide, tall], [WIDE, TALL], [], 10**9, "other_rows",
        aliases={1: 0, 2: 1},
    )


def gradients(stage, meta, arrays, state, dtype):
    share = ((KEYS // NX, 2 * WIDTH), dtype)
    count = 1 + len(arrays)
    return run(
        functools.partial(gradients_kernel, stage),
        [meta],
        arrays + list(state),
        [SUMS, DQT] + [share] * len(STAGES[stage]),
        [pltpu.VMEM((1, COLS), F32)] * 2,
        8 * 10**9,
        "gradients",
        aliases={count: 0, count + 1: 1},
    )


def per_device(queries, keys, values, forward_out, out_grad, span_ids):
    me = lax.axis_index("ctx")
    my_x, my_z, my_y = me // (NZ * NY), (me // NY) % NZ, me % NY
    where = jnp.stack([my_x, my_z, my_y]).astype(jnp.int32)
    carried = ((SPAN + 16, 2 * WIDTH), BF16)
    sem = pltpu.SemaphoreType.DMA
    local = pltpu.VMEM((2 * SPAN, WIDTH), BF16)
    kept, sent = run(
        pack_kernel, [span_ids, where], [keys, values], [carried] * 2, [local, local, sem, sem],
        10, "pack", far=(0, 1),
    )
    given = shift(sent, dy=1)
    block, meta = run(
        join_kernel, [span_ids, where], [kept, given],
        [((BLOCK, 2 * WIDTH), BF16), ((5,), jnp.int32)], [], 10, "join", scalar_outs=(1,),
    )

    block, queries, out_grad, forward_out = lax.optimization_barrier(
        (block, queries, out_grad, forward_out)
    )
    q_other = shift(queries, dy=1)
    g_other = shift(out_grad, dy=1)
    qs, gs, qt, gt, delta = run(
        own_rows_kernel, [], [queries, out_grad, forward_out],
        [WIDE, WIDE, TALL, TALL, ((8, COLS // 2), F32)], [], 10**9, "own_rows",
    )
    below, above, across = shift(block, dz=1), shift(block, dz=-1), shift(block, dz=NZ // 2)
    below, above, across, qs, gs, qt, gt, delta = lax.optimization_barrier(
        (below, above, across, qs, gs, qt, gt, delta)
    )
    further = [
        shift(jnp.concatenate([across, below], axis=0), dz=1),
        shift(jnp.concatenate([across, above], axis=0), dz=-1),
    ]
    (plane,) = run(
        plane_kernel, [], [block, across, below, above] + further,
        [((2 * NZ * SPAN + 16, 2 * WIDTH), BF16)], [], 10, "plane",
    )
    qs, qt = other_rows(q_other, qs, qt)
    gs, gt = other_rows(g_other, gs, gt)
    near, far, back = (shift(plane, dx=d) for d in range(1, NX))
    gathered = [plane, near, back, far]
    stats = None
    for i, part in enumerate(gathered):
        last = i == len(gathered) - 1
        stats = statistics(meta, [part], qt, stats, delta if last else None)
    other_stats = shift(stats, dy=1)
    pairs, *state = run(
        functools.partial(sort_kernel, len(gathered)), [], gathered,
        [((KEYS, 2 * WIDTH), BF16), SUMS, DQT], [], 10**9, "sort",
    )

    arrays = [pairs, qs, gs, qt, gt, stats, other_stats]
    *state, far = gradients(0, meta, arrays, state, BF16)
    far = shift(far, dx=ORDER[0])
    *state, up, down = gradients(1, meta, arrays, state, BF16)
    up, down = shift(up, dx=1), shift(down, dx=-1)
    far, *state = lax.optimization_barrier((far, *state))
    *state, own = gradients(2, meta, arrays, state, F32)
    dqt = state[1]
    over_x = [own, far, up, down]
    dq_own, dq_sent = run(
        d_queries_kernel, [], [dqt], [(OWN, F32), (OWN, BF16)], [], 10**8, "d_queries"
    )

    over_x = sum(part.astype(F32) for part in over_x)
    over_x, dq_own, dq_sent = lax.optimization_barrier((over_x, dq_own, dq_sent))
    pair = 2 * SPAN
    mine, across, above, below, up, down = (
        over_x[a * pair : b * pair] for a, b in ((0, 1), (1, 2), (2, 3), (3, 4), (4, 6), (6, 8))
    )
    from_below = shift(up.astype(BF16), dz=1).astype(F32)
    from_above = shift(down.astype(BF16), dz=-1).astype(F32)
    across = across + from_below[:pair] + from_above[:pair]
    above = above + from_below[pair:]
    below = below + from_above[pair:]
    over_z = mine
    for part, d in ((across, NZ // 2), (above, 1), (below, -1)):
        over_z = over_z + shift(part.astype(BF16), dz=d).astype(F32)
    dq_given = shift(dq_sent, dy=1)
    over_z, dq_given = lax.optimization_barrier((over_z, dq_given))
    d_queries = (dq_own + dq_given.astype(F32)).astype(BF16)
    first = my_y == 0
    upper, lower = over_z[:SPAN], over_z[SPAN:]
    given = shift(jnp.where(first, lower, upper), dy=1)
    final = jnp.where(
        first,
        jnp.concatenate([upper, given], axis=0),
        jnp.concatenate([given, lower], axis=0),
    )
    return (d_queries, final[:, :WIDTH] * FACTOR, final[:, WIDTH:])


def solution(mesh):
    rows = P(("dp", "ctx"), None)
    return jax.shard_map(
        per_device,
        mesh=mesh,
        in_specs=(rows, rows, rows, rows, rows, P(("dp", "ctx"))),
        out_specs=(rows, rows, rows),
        check_vma=False,
    )
```

```python
import functools
import math

import jax
import jax.numpy as jnp
from jax import lax
from jax.experimental import pallas as pl
from jax.experimental.pallas import tpu as pltpu
from jax.sharding import PartitionSpec as P

NX, NZ, NY = 4, 8, 2
DEVICES = NX * NZ * NY
SPAN = 64
SPANS = 2 * DEVICES
WIDTH = 128
HEADS = 12
ROWS = HEADS * SPAN
KINDS = 2 * NY
COLS = KINDS * ROWS
KEYS = SPANS // NY * SPAN
STATS_TILE = 8 * SPAN
TILE = 8 * SPAN
BLOCK = 2 * SPAN + 16
FACTOR = 1.0 / math.sqrt(WIDTH)
SCALE = FACTOR * math.log2(math.e)
NEG = -1e30
SAFE = 64.0
VMEM_LIMIT = 28 * 1024 * 1024

F32 = jnp.float32
BF16 = jnp.bfloat16


def place(x, z, y):
    return ((x % NX) * NZ + z % NZ) * NY + y % NY


def shift(block, dx=0, dz=0, dy=0):
    pairs = [
        (place(x, z, y), place(x + dx, z + dz, y + dy))
        for x in range(NX)
        for z in range(NZ)
        for y in range(NY)
    ]
    return lax.ppermute(block, "ctx", pairs)


def spans_of(meta):
    return meta[0], SPANS - 1 - meta[0], meta[1], SPANS - 1 - meta[1]


def pick(spans, kind):
    result = spans[0]
    for i in range(1, KINDS):
        result = jnp.where(kind == i, spans[i], result)
    return result


def columns(start, width=ROWS):
    return pl.ds(pl.multiple_of(start, WIDTH), width)


def numbers_rows(first, second):
    index = lax.broadcasted_iota(jnp.int32, (16, 2 * WIDTH), 0)
    return jnp.where(index < 8, first, second).astype(F32).astype(BF16)


def pack_kernel(ids, where, keys_any, values_any, kept, sent, keys, values, sem, sem_v):
    copies = [
        pltpu.make_async_copy(keys_any, keys, sem),
        pltpu.make_async_copy(values_any, values, sem_v),
    ]
    for copy in copies:
        copy.start()
    for copy in copies:
        copy.wait()
    keep = jnp.where((ids[0] & 1) == where[2], 0, 1)
    for target, slot in ((kept, keep), (sent, 1 - keep)):
        rows = pl.ds(pl.multiple_of(slot * SPAN, SPAN), SPAN)
        target[:SPAN, :WIDTH] = keys[rows, :]
        target[:SPAN, WIDTH:] = values[rows, :]
        number = jnp.where(slot == 0, ids[0], ids[1])
        target[SPAN:, :] = numbers_rows(number, ids[0])


def join_kernel(ids, where, kept, given, block, meta):
    block[:SPAN, :] = kept[:SPAN, :]
    block[SPAN : 2 * SPAN, :] = given[:SPAN, :]
    mine, other = kept[SPAN:, :].astype(F32), given[SPAN:, :].astype(F32)
    block[2 * SPAN :, :] = jnp.concatenate([mine[:8], other[:8]], axis=0).astype(BF16)
    meta[0] = ids[0]
    meta[1] = other[8, 0].astype(jnp.int32)
    for i in range(3):
        meta[2 + i] = where[i]


def place_heads(own, refs, sources):
    for slot in range(2):
        rows = slice(slot * SPAN, (slot + 1) * SPAN)
        for b in range(HEADS // 2):
            lanes = [slice(h * WIDTH, (h + 1) * WIDTH) for h in (2 * b, 2 * b + 1)]
            start = ((0 if own else 2) + slot) * ROWS + b * WIDTH
            target = slice(start, start + WIDTH)
            blocks = []
            for source in sources:
                blocks.append(jnp.concatenate([source[rows, i] for i in lanes], axis=0))
            for (tall, wide), block in zip(refs, blocks):
                wide[target, :] = block
                tall[:, target] = block.T
            if own:
                yield target, blocks


def own_rows_kernel(q_own, g_own, o_own, qs, gs, qt, gt, delta):
    for target, (_, g, o) in place_heads(True, ((qt, qs), (gt, gs)), (q_own, g_own, o_own)):
        total = jnp.sum((g.astype(F32) * o.astype(F32)).T, axis=0, keepdims=True)
        delta[:, target] = jnp.broadcast_to(total, (8, WIDTH))


def other_rows_kernel(rows, _wide, _tall, wide, tall):
    for _ in place_heads(False, ((tall, wide),), (rows,)):
        pass


def plane_kernel(*refs):
    pieces, plane = refs[:-1], refs[-1]
    index = lax.broadcasted_iota(jnp.int32, (16, 2 * WIDTH), 0)
    numbers = jnp.zeros((16, 2 * WIDTH), F32)
    count = 0
    for piece in pieces:
        for b in range(piece.shape[0] // BLOCK):
            start = b * BLOCK
            plane[count * SPAN : (count + 2) * SPAN, :] = piece[start : start + 2 * SPAN, :]
            tail = piece[start + 2 * SPAN : start + BLOCK, :].astype(F32)
            numbers = jnp.where(index == count, tail[0:1], numbers)
            numbers = jnp.where(index == count + 1, tail[8:9], numbers)
            count += 2
    plane[count * SPAN :, :] = numbers.astype(BF16)


def read_numbers(parts):
    found = []
    for part in parts:
        tail = part[2 * NZ * SPAN :, :WIDTH].astype(F32)
        for i in range(2 * NZ):
            found.append((tail[i, 0].astype(jnp.int32), part, i * SPAN))
    return found


def sort_kernel(n_parts, *refs):
    parts, (pairs, sums, dqt) = refs[:n_parts], refs[n_parts:]
    sums[...] = jnp.zeros(sums.shape, F32)
    dqt[...] = jnp.zeros(dqt.shape, F32)
    for number, part, row in read_numbers(parts):
        target = pl.multiple_of(number // NY * SPAN, SPAN)
        pairs[pl.ds(target, SPAN), :] = part[row : row + SPAN, :]


def hide(scores, offsets):
    shape = (scores.shape[0], WIDTH)
    index = lax.broadcasted_iota(jnp.int32, shape, 0)
    offset = jnp.full(shape, offsets[0], jnp.int32)
    for i in range(1, len(offsets)):
        offset = jnp.where(index >= i * SPAN, offsets[i], offset)
    row = lax.broadcasted_iota(jnp.int32, shape, 1) & (SPAN - 1)
    lowered = jnp.where(offset * SPAN + (index & (SPAN - 1)) > row, 2 * NEG, 0.0)
    return scores + jnp.concatenate([lowered] * (scores.shape[1] // WIDTH), axis=1)


def statistics_kernel(n_parts, first, last, meta, *refs):
    parts, refs = refs[:n_parts], list(refs[n_parts:])
    qt = refs.pop(0)
    before_ref = None if first else refs.pop(0)
    delta = refs.pop(0) if last else None
    out, row_max, row_sum, base, top, extra, keys, ordered = refs
    spans = spans_of(meta)
    found = read_numbers(parts)
    for number, part, row in found:
        rank = sum((other < number).astype(jnp.int32) for other, _, _ in found)
        ordered[rank] = number
        target = pl.multiple_of(rank * SPAN, SPAN)
        keys[pl.ds(target, SPAN), :] = part[row : row + SPAN, :WIDTH]
    if first:
        row_max[...] = jnp.full((8, COLS), NEG, F32)
        row_sum[...] = jnp.zeros((8, COLS), F32)
    else:
        row_max[...] = before_ref[:8, :]
        row_sum[...] = before_ref[8:, :]
    group = STATS_TILE // SPAN

    def visit_all(visit, width, always_masked):
        def step(i, carry):
            kind = i // (ROWS // width)
            span = pick(spans, kind)
            cols = columns(i * width, width)

            def scores(tile, masked):
                k = keys[pl.ds(pl.multiple_of(tile * STATS_TILE, STATS_TILE), STATS_TILE), :]
                s = jnp.dot(k, qt[:, cols], preferred_element_type=F32) * SCALE
                if masked:
                    offsets = [ordered[tile * group + i] - span for i in range(group)]
                    s = hide(s, offsets)
                visit(s.reshape(STATS_TILE // 8, 8, width), cols)

            full = sum((number < span).astype(jnp.int32) for number, _, _ in found) // group
            seen = sum((number <= span).astype(jnp.int32) for number, _, _ in found)
            if always_masked:
                tiles = (seen + group - 1) // group
                lax.fori_loop(0, tiles, lambda t, c: scores(t, True), None)
                return carry
            lax.fori_loop(0, full, lambda t, c: scores(t, False), None)

            @pl.when(seen > full * group)
            def _():
                scores(full, True)

            return carry

        lax.fori_loop(0, COLS // width, step, 0)

    def against_base(s, cols):
        top[:, cols] = jnp.maximum(top[:, cols], jnp.max(s, axis=0))
        extra[:, cols] += jnp.sum(jnp.exp2(s - base[:, cols][None]), axis=0)

    def against_maximum(s, cols):
        before = row_max[:, cols]
        after = jnp.maximum(before, jnp.max(s, axis=0))
        fresh = jnp.sum(jnp.exp2(s - after[None]), axis=0)
        row_sum[:, cols] = row_sum[:, cols] * jnp.exp2(before - after) + fresh
        row_max[:, cols] = after

    unset = row_max[...] <= NEG
    base[...] = jnp.where(unset, 0.0, row_max[...])
    top[...] = jnp.full((8, COLS), 2 * NEG, F32)
    extra[...] = jnp.zeros((8, COLS), F32)
    visit_all(against_base, ROWS, False)
    unset = row_max[...] <= NEG
    seen = top[...] > NEG
    gap = top[...] - base[...]
    far = seen & ((gap > SAFE) | (unset & (gap < -SAFE)))
    any_far = jnp.max(jnp.where(far, 1.0, 0.0)) > 0.0

    @pl.when(jnp.logical_not(any_far))
    def _():
        empty = unset & jnp.logical_not(seen)
        after = jnp.maximum(base[...], top[...])
        total = (row_sum[...] + extra[...]) * jnp.exp2(base[...] - after)
        row_sum[...] = jnp.where(empty, 0.0, total)
        row_max[...] = jnp.where(empty, NEG, after)

    @pl.when(any_far)
    def _():
        visit_all(against_maximum, WIDTH, True)

    if not last:
        out[:8, :] = row_max[...]
        out[8:, :] = row_sum[...]
    else:
        most = jnp.max(row_max[...], axis=0, keepdims=True)
        total = jnp.sum(row_sum[...] * jnp.exp2(row_max[...] - most), axis=0, keepdims=True)
        out[0:1, :] = most
        out[1:2, :] = total
        out[2:3, : 2 * ROWS] = delta[0:1, :]
        out[2:3, 2 * ROWS :] = jnp.zeros((1, 2 * ROWS), F32)
        out[3:8, :] = jnp.zeros((5, COLS), F32)


ORDER = (2, 1, NX - 1, 0)
TILES = KEYS // NX // TILE
STAGES = ((0,), (1, 2), (3,))


Z_ORDER = (0, 4, 1, 7, 5, 2, 3, 6)


def gradients_kernel(stage, meta, pairs, qs, gs, qt, gt, mine_ref, other_ref, _sums, _dqt, *refs):
    sums, dqt = refs[:2]
    outs, (level, delta) = refs[2:-2], refs[-2:]
    spans = spans_of(meta)
    my_x, my_z, parity = meta[2], meta[3], meta[4]
    half = 2 * ROWS
    for mine, other in ((slice(0, half), slice(half, COLS)), (slice(half, COLS), slice(0, half))):
        top = jnp.maximum(mine_ref[0:1, mine], other_ref[0:1, other])
        total = mine_ref[1:2, mine] * jnp.exp2(mine_ref[0:1, mine] - top)
        total += other_ref[1:2, other] * jnp.exp2(other_ref[0:1, other] - top)
        level[:, mine] = top + jnp.log2(total)
        delta[:, mine] = mine_ref[2:3, mine] + other_ref[2:3, other]
    group = TILE // SPAN
    lasts = [jnp.maximum(span - parity, 0) // NY // group for span in spans]
    firsts = [(my_x + off) % NX * TILES for off in ORDER]
    counts = [
        sum(jnp.clip(last - first + 1, 0, TILES) for last in lasts) for first in firsts
    ]
    ready = [sum(counts[: entries[-1] + 1]) for entries in STAGES]
    everything = ready[-1]
    ends = [
        jnp.maximum(needed, (everything * (i + 1) + len(STAGES) - 1) // len(STAGES))
        for i, needed in enumerate(ready)
    ]
    begin = 0 if stage == 0 else ends[stage - 1]
    end = ends[stage]

    def visit(kind, tile, masked):
        span = pick(spans, kind)
        cols = columns(kind * ROWS)
        rows = pl.ds(pl.multiple_of(tile * TILE, TILE), TILE)
        k = pairs[rows, :WIDTH]
        v = pairs[rows, WIDTH:]
        s = jnp.dot(k, qt[:, cols], preferred_element_type=F32) * SCALE
        if masked:
            s = hide(s, [(tile * group + j) * NY + parity - span for j in range(group)])
        p = jnp.exp2(s - level[:, cols])
        dp = jnp.dot(v, gt[:, cols], preferred_element_type=F32)
        ds = (p * (dp - delta[:, cols])).astype(BF16)
        d_value = jnp.dot(p.astype(BF16), gs[cols, :], preferred_element_type=F32)
        d_key = jnp.dot(ds, qs[cols, :], preferred_element_type=F32)
        dqt[:, cols] += jnp.dot(k.T, ds, preferred_element_type=F32)
        sums[rows, :WIDTH] += d_key
        sums[rows, WIDTH:] += d_value

    def step(i, done):
        entry, kind = i // KINDS, i % KINDS
        first, last = pick(firsts, entry), pick(lasts, kind)
        count = jnp.clip(last - first + 1, 0, TILES)

        def part_step(part, carry):
            tile = first + part

            @pl.when(tile < last)
            def _():
                visit(kind, tile, False)

            @pl.when(tile == last)
            def _():
                visit(kind, tile, True)

            return carry

        low, high = jnp.clip(begin - done, 0, count), jnp.clip(end - done, 0, count)
        lax.fori_loop(low, high, part_step, 0)
        return done + count

    lax.fori_loop(0, len(ORDER) * KINDS, step, jnp.int32(0))
    pair = 2 * SPAN
    for entry, out in zip(STAGES[stage], outs):
        for i, z_off in enumerate(Z_ORDER):
            start = firsts[entry] * TILE + (my_z + z_off) % NZ * pair
            source = pl.ds(pl.multiple_of(start, pair), pair)
            out[i * pair : (i + 1) * pair, :] = sums[source, :].astype(out.dtype)


def d_queries_kernel(dqt, dq_own, dq_other):
    for device, out in enumerate((dq_own, dq_other)):
        for slot in range(2):
            for b in range(ROWS // WIDTH):
                start = (2 * device + slot) * ROWS + b * WIDTH
                block = dqt[:, start : start + WIDTH].T * FACTOR
                for half in range(2):
                    h = 2 * b + half
                    out[slot * SPAN : (slot + 1) * SPAN, h * WIDTH : (h + 1) * WIDTH] = block[
                        half * SPAN : (half + 1) * SPAN
                    ].astype(out.dtype)


def run(kernel, scalars, arrays, outs, scratch, flops, name, far=(), aliases=None, scalar_outs=()):
    spaces = [pltpu.SMEM] * len(scalars)
    spaces += [pltpu.HBM if i in far else pltpu.VMEM for i in range(len(arrays))]
    return pl.pallas_call(
        kernel,
        out_shape=[jax.ShapeDtypeStruct(s, d) for s, d in outs],
        in_specs=[pl.BlockSpec(memory_space=space) for space in spaces],
        out_specs=[
            pl.BlockSpec(memory_space=pltpu.SMEM if i in scalar_outs else pltpu.VMEM)
            for i in range(len(outs))
        ],
        scratch_shapes=scratch,
        input_output_aliases=aliases or {},
        compiler_params=pltpu.CompilerParams(vmem_limit_bytes=VMEM_LIMIT),
        cost_estimate=pl.CostEstimate(flops=flops, bytes_accessed=10**5, transcendentals=0),
        name=name,
    )(*scalars, *arrays)


WIDE = ((COLS, WIDTH), BF16)
TALL = ((WIDTH, COLS), BF16)
FLAT = ((8, COLS), F32)
OWN = (2 * SPAN, HEADS * WIDTH)
SUMS = ((KEYS, 2 * WIDTH), F32)
DQT = ((WIDTH, COLS), F32)


def statistics(meta, parts, qt, before, delta):
    first, last = before is None, delta is not None
    count = 2 * NZ * len(parts)
    arrays = list(parts) + [qt] + [a for a in (before, delta) if a is not None]
    return run(
        functools.partial(statistics_kernel, len(parts), first, last),
        [meta],
        arrays,
        [FLAT if last else ((16, COLS), F32)],
        [pltpu.VMEM((8, COLS), F32)] * 5
        + [pltpu.VMEM((count * SPAN, WIDTH), BF16), pltpu.SMEM((count,), jnp.int32)],
        2 * 10**9,
        "row_statistics",
    )[0]


def other_rows(rows, wide, tall):
    return run(
        other_rows_kernel, [], [rows, wide, tall], [WIDE, TALL], [], 10**9, "other_rows",
        aliases={1: 0, 2: 1},
    )


def gradients(stage, meta, arrays, state, dtype):
    share = ((KEYS // NX, 2 * WIDTH), dtype)
    count = 1 + len(arrays)
    return run(
        functools.partial(gradients_kernel, stage),
        [meta],
        arrays + list(state),
        [SUMS, DQT] + [share] * len(STAGES[stage]),
        [pltpu.VMEM((1, COLS), F32)] * 2,
        8 * 10**9,
        "gradients",
        aliases={count: 0, count + 1: 1},
    )


def per_device(queries, keys, values, forward_out, out_grad, span_ids):
    me = lax.axis_index("ctx")
    my_x, my_z, my_y = me // (NZ * NY), (me // NY) % NZ, me % NY
    where = jnp.stack([my_x, my_z, my_y]).astype(jnp.int32)
    carried = ((SPAN + 16, 2 * WIDTH), BF16)
    sem = pltpu.SemaphoreType.DMA
    local = pltpu.VMEM((2 * SPAN, WIDTH), BF16)
    kept, sent = run(
        pack_kernel, [span_ids, where], [keys, values], [carried] * 2, [local, local, sem, sem],
        10, "pack", far=(0, 1),
    )
    given = shift(sent, dy=1)
    block, meta = run(
        join_kernel, [span_ids, where], [kept, given],
        [((BLOCK, 2 * WIDTH), BF16), ((5,), jnp.int32)], [], 10, "join", scalar_outs=(1,),
    )

    block, queries, out_grad, forward_out = lax.optimization_barrier(
        (block, queries, out_grad, forward_out)
    )
    q_other = shift(queries, dy=1)
    g_other = shift(out_grad, dy=1)
    qs, gs, qt, gt, delta = run(
        own_rows_kernel, [], [queries, out_grad, forward_out],
        [WIDE, WIDE, TALL, TALL, ((8, COLS // 2), F32)], [], 10**9, "own_rows",
    )
    below, above, across = shift(block, dz=1), shift(block, dz=-1), shift(block, dz=NZ // 2)
    below, above, across, qs, gs, qt, gt, delta = lax.optimization_barrier(
        (below, above, across, qs, gs, qt, gt, delta)
    )
    further = [
        shift(jnp.concatenate([across, below], axis=0), dz=1),
        shift(jnp.concatenate([across, above], axis=0), dz=-1),
    ]
    (plane,) = run(
        plane_kernel, [], [block, across, below, above] + further,
        [((2 * NZ * SPAN + 16, 2 * WIDTH), BF16)], [], 10, "plane",
    )
    qs, qt = other_rows(q_other, qs, qt)
    gs, gt = other_rows(g_other, gs, gt)
    near, far, back = (shift(plane, dx=d) for d in range(1, NX))
    gathered = [plane, near, back, far]
    stats = None
    for parts in ([plane], [near], [back, far]):
        stats = statistics(meta, parts, qt, stats, delta if len(parts) == 2 else None)
    other_stats = shift(stats, dy=1)
    pairs, *state = run(
        functools.partial(sort_kernel, len(gathered)), [], gathered,
        [((KEYS, 2 * WIDTH), BF16), SUMS, DQT], [], 10**9, "sort",
    )

    arrays = [pairs, qs, gs, qt, gt, stats, other_stats]
    *state, far = gradients(0, meta, arrays, state, BF16)
    far = shift(far, dx=ORDER[0])
    *state, up, down = gradients(1, meta, arrays, state, BF16)
    up, down = shift(up, dx=1), shift(down, dx=-1)
    far, *state = lax.optimization_barrier((far, *state))
    *state, own = gradients(2, meta, arrays, state, F32)
    dqt = state[1]
    over_x = [own, far, up, down]
    dq_own, dq_sent = run(
        d_queries_kernel, [], [dqt], [(OWN, F32), (OWN, BF16)], [], 10**8, "d_queries"
    )

    over_x = sum(part.astype(F32) for part in over_x)
    over_x, dq_own, dq_sent = lax.optimization_barrier((over_x, dq_own, dq_sent))
    pair = 2 * SPAN
    mine, across, above, below, up, down = (
        over_x[a * pair : b * pair] for a, b in ((0, 1), (1, 2), (2, 3), (3, 4), (4, 6), (6, 8))
    )
    from_below = shift(up.astype(BF16), dz=1).astype(F32)
    from_above = shift(down.astype(BF16), dz=-1).astype(F32)
    across = across + from_below[:pair] + from_above[:pair]
    above = above + from_below[pair:]
    below = below + from_above[pair:]
    over_z = mine
    for part, d in ((across, NZ // 2), (above, 1), (below, -1)):
        over_z = over_z + shift(part.astype(BF16), dz=d).astype(F32)
    dq_given = shift(dq_sent, dy=1)
    over_z, dq_given = lax.optimization_barrier((over_z, dq_given))
    d_queries = (dq_own + dq_given.astype(F32)).astype(BF16)
    first = my_y == 0
    upper, lower = over_z[:SPAN], over_z[SPAN:]
    given = shift(jnp.where(first, lower, upper), dy=1)
    final = jnp.where(
        first,
        jnp.concatenate([upper, given], axis=0),
        jnp.concatenate([given, lower], axis=0),
    )
    return (d_queries, final[:, :WIDTH] * FACTOR, final[:, WIDTH:])


def solution(mesh):
    rows = P(("dp", "ctx"), None)
    return jax.shard_map(
        per_device,
        mesh=mesh,
        in_specs=(rows, rows, rows, rows, rows, P(("dp", "ctx"))),
        out_specs=(rows, rows, rows),
        check_vma=False,
    )
```
